256 devices in a mesh: ep: 32 (over z, y_lo, core), fsdp: 8 (over y_hi, x).
Axes of the slice: x: 4, y: 4 (y_hi: 2, y_lo: 2; y = y_hi * 2 + y_lo), z: 8, core: 2. Of those that a mesh axis runs over, the one named last changes fastest.
Arguments:
- tokens: bfloat16 [4096, 7168], P('ep', 'fsdp'), may hold values from -6 to 6
- cotangent: bfloat16 [4096, 7168], P('ep', 'fsdp'), may hold values from -6 to 6
- route_gates: float32 [4096, 2], P('ep'), may hold values from 0.2 to 1
- expert_ids: int32 [4096, 2], P('ep'), may hold values from 0 to 7, all different within a row; in each aligned block of 128 rows (0 to 127, 128 to 255, ...) at most 64 rows name the same one
- w_gate: bfloat16 [7168, 8192], P('fsdp', 'ep'), may hold values from -0.0625 to 0.0625
- w_up: bfloat16 [7168, 8192], P('fsdp', 'ep'), may hold values from -0.0625 to 0.0625
- w_down: bfloat16 [7168, 8192], P('fsdp', 'ep'), may hold values from -0.1875 to 0.1875
Outputs:
- grad_tokens: bfloat16 [4096, 7168], P('ep', 'fsdp')
- grad_gate: bfloat16 [7168, 8192], P('fsdp', 'ep')
- grad_up: bfloat16 [7168, 8192], P('fsdp', 'ep')
- grad_down: bfloat16 [7168, 8192], P('fsdp', 'ep')
The draws below stay inside these ranges and needn't reach their ends.
Inputs may be any that keep to these rules, and one draw needn't show every extreme that they name: `expert_ids`: each token names 2 different experts; among the 128 tokens of one block no expert is named more than 64 times, a bound that some block reaches.
All inputs are finite; a program needn't handle non-finite values.
Results may differ from the reference program's by a relative error of at most 0.0064.
Values may be sent and summed in bfloat16 or wider, within the bound.
A program may use at most 64 MiB of HBM per device.

```python
import math
import jax
import jax.numpy as jnp
import numpy as np
from jax import lax

D = 7168
H_EXP = 1024
EXPERTS = 8
TOP = 2
TOK_DEV = 128
CAP = 64
HID_DEV = 256
TOKENS = 4096
N_EP = 32


def steps_of(key, shape, cuts, smallest, top_value):
    factor_of = 1.0
    for dim, blocks in cuts:
        heights = jax.random.uniform(jax.random.fold_in(jax.random.fold_in(key, 6), dim), (blocks,), jnp.float32, smallest / len(cuts), top_value / len(cuts))
        factor_of = factor_of * jnp.repeat(jnp.exp(heights), shape[dim] // blocks).reshape((-1,) + (1,) * (len(shape) - 1 - dim))
    return factor_of


def assign_block(rng, own, number, rows, number_of, top, reach, lean):
    order = jax.random.permutation(rng, number_of)
    heavy_load, common = load_shares(number_of, rows * top, reach, lean, True), load_shares(number_of, rows * top, reach, lean, False)
    places = jnp.arange(number_of)

    def named(sizes, rotation):
        used = int((sizes > 0).sum())
        fixed = max(1, used // 4)
        shifted = fixed + (places - fixed + rotation * (used - fixed)) % max(1, number_of - fixed)
        return jnp.zeros((number_of,), jnp.int32).at[order[jnp.where(places < fixed, places, shifted)]].set(jnp.asarray(sizes, jnp.int32))

    sizes = jnp.where(number % 4 == 0, named(heavy_load, number // 4), named(common, number - number // 4 - 1))
    mixed = jax.random.permutation(jax.random.fold_in(own, 3), number_of)
    source_of, sink = mixed[0:number_of // 2 * 2:2], mixed[1:number_of // 2 * 2:2]
    margin = jnp.minimum(sizes[source_of] - 1, reach - sizes[sink]) // 2
    margin = jnp.where((source_of == order[0]) | (sink == order[0]) | (sizes[sink] == 0), 0, jnp.maximum(margin, 0))
    shifted = jax.random.randint(jax.random.fold_in(own, 4), (number_of // 2,), 0, 1 << 20) % (margin + 1)
    sizes = sizes.at[source_of].add(-shifted).at[sink].add(shifted)
    members = jnp.searchsorted(jnp.cumsum(sizes), jnp.arange(rows * top), side="right").astype(jnp.int32)
    table = members.reshape(top, rows).T
    table = table[jax.random.permutation(jax.random.fold_in(own, 1), rows)]
    rotation = jax.random.randint(jax.random.fold_in(own, 2), (rows, 1), 0, top)
    return jnp.take_along_axis(table, (jnp.arange(top)[None, :] + rotation) % top, axis=1)


def load_shares(number_of, total, limit, slope, full):
    portions = [(1 << 20) // math.isqrt(rank ** slope) + 1 for rank in range(1, number_of + 1)]
    largest = limit if full else min(limit, max(-(-total // number_of), total * portions[0] // sum(portions)))
    least = 1 if total - largest >= number_of - 1 else 0
    given, spare = [largest] + [least] * (number_of - 1), total - largest - least * (number_of - 1)
    while spare > 0:
        candidates = [i for i in range(1, number_of) if given[i] < largest] or [i for i in range(1, number_of) if given[i] < limit]
        pool, left = sum([portions[i] for i in candidates]), spare
        for i in candidates:
            addition = min(limit - given[i], max(1, left * portions[i] // pool), spare)
            given[i] = given[i] + addition
            spare = spare - addition
    return np.array(given)


def scatter_about(stream_key, shape, spread, reach, pieces=(), kind=jnp.bfloat16):
    array = spread * jax.random.normal(stream_key, shape, jnp.float32)
    if pieces:
        array = array * steps_of(stream_key, shape, pieces, -0.22, 0.18)
    return jnp.clip(array, -reach, reach).astype(kind)


def setup_inputs(seed: int = 0) -> dict:
    streams_of = jax.random.split(jax.random.key(seed), 8)
    tokens = scatter_about(streams_of[0], (TOKENS, D), 1.0, 6.0, ((0, 32), (1, 8)))
    cotangent = scatter_about(streams_of[1], (TOKENS, D), 1.0, 6.0, ((0, 32), (1, 8)))
    route_gates = jnp.clip(0.2 + 0.8 * jax.random.uniform(streams_of[2], (TOKENS, TOP), jnp.float32) ** steps_of(streams_of[2], (TOKENS, TOP), ((0, 32),), -0.2, 0.2), 0.2, 1.0)
    expert_ids_keys = jax.random.split(jax.random.fold_in(streams_of[3], 1), TOKENS // TOK_DEV)
    expert_ids_turns = jax.random.permutation(jax.random.fold_in(streams_of[3], 3), TOKENS // TOK_DEV)
    expert_ids = jax.vmap(lambda own, number: assign_block(jax.random.fold_in(streams_of[3], 2), own, number, TOK_DEV, EXPERTS, TOP, CAP, 2))(expert_ids_keys, expert_ids_turns).reshape((TOKENS, TOP))
    w_gate = scatter_about(streams_of[4], (D, EXPERTS * H_EXP), D ** -0.5, 0.0625, ((0, 8), (1, 32)))
    w_up = scatter_about(streams_of[5], (D, EXPERTS * H_EXP), D ** -0.5, 0.0625, ((0, 8), (1, 32)))
    w_down = scatter_about(streams_of[6], (D, EXPERTS * H_EXP), H_EXP ** -0.5, 0.1875, ((0, 8), (1, 32)))
    return {"tokens": tokens, "cotangent": cotangent, "route_gates": route_gates, "expert_ids": expert_ids, "w_gate": w_gate, "w_up": w_up, "w_down": w_down}


def cross_dot(left, right):
    return lax.dot_general(left, right, (((0,), (0,)), ((), ())), preferred_element_type=jnp.float32)


def right_dot(left, right):
    return lax.dot_general(left, right, (((1,), (1,)), ((), ())), preferred_element_type=jnp.float32)


def reference(tokens, cotangent, route_gates, expert_ids, w_gate, w_up, w_down):
    block_count = N_EP
    pair_count = TOK_DEV * TOP
    split_ways = N_EP // EXPERTS
    flat_ids = expert_ids.reshape(block_count, pair_count)
    onehot = (flat_ids[:, :, None] == jnp.arange(EXPERTS, dtype=jnp.int32)[None, None, :]).astype(jnp.int32)
    slot_index = jnp.sum(jnp.cumsum(onehot, axis=1) * onehot, axis=2) - 1
    destination = (flat_ids * CAP + slot_index).astype(jnp.int32)
    table = jnp.full((block_count, EXPERTS * CAP), -1, jnp.int32)
    table = table.at[jnp.arange(block_count, dtype=jnp.int32)[:, None], destination].set(
        jnp.broadcast_to(jnp.arange(pair_count, dtype=jnp.int32)[None, :], (block_count, pair_count)))
    gate_flat = route_gates.reshape(block_count * pair_count)
    row_count = N_EP * CAP

    def piece_step(grad_acc, piece_id):
        expert = piece_id // split_ways
        column = (piece_id * HID_DEV).astype(jnp.int32)
        gate_piece = lax.dynamic_slice_in_dim(w_gate, column, HID_DEV, 1)
        up_piece = lax.dynamic_slice_in_dim(w_up, column, HID_DEV, 1)
        down_piece = lax.dynamic_slice_in_dim(w_down, column, HID_DEV, 1)
        slot_ids = lax.dynamic_slice_in_dim(table, (expert * CAP).astype(jnp.int32), CAP, 1)
        filled = slot_ids >= 0
        safe_ids = jnp.where(filled, slot_ids, 0)
        block_ids = jnp.arange(N_EP, dtype=jnp.int32)
        token_rows = (block_ids[:, None] * TOK_DEV + safe_ids // TOP).reshape(row_count)
        pair_rows = (block_ids[:, None] * pair_count + safe_ids).reshape(row_count)
        filled = filled.reshape(row_count)
        weight = jnp.where(filled, gate_flat[pair_rows], jnp.float32(0.0))
        rows_x = jnp.where(filled[:, None], tokens[token_rows], jnp.zeros((), jnp.bfloat16))
        rows_c = (weight[:, None] * cotangent[token_rows].astype(jnp.float32)).astype(jnp.bfloat16)
        pre_gate = jnp.dot(rows_x, gate_piece, preferred_element_type=jnp.float32)
        pre_up = jnp.dot(rows_x, up_piece, preferred_element_type=jnp.float32)
        sigmoid_gate = jax.nn.sigmoid(pre_gate)
        activated = pre_gate * sigmoid_gate
        hidden = (activated * pre_up).astype(jnp.bfloat16)
        grad_hidden = jnp.dot(rows_c, down_piece, preferred_element_type=jnp.float32)
        grad_a = (grad_hidden * pre_up * sigmoid_gate * (1.0 + pre_gate * (1.0 - sigmoid_gate))).astype(jnp.bfloat16)
        grad_u = (grad_hidden * activated).astype(jnp.bfloat16)
        row_term = (right_dot(grad_a, gate_piece) + right_dot(grad_u, up_piece)).astype(jnp.bfloat16)
        grad_acc = grad_acc.at[token_rows].add(row_term.astype(jnp.float32))
        sum_gate = cross_dot(rows_x, grad_a).astype(jnp.bfloat16)
        sum_up = cross_dot(rows_x, grad_u).astype(jnp.bfloat16)
        sum_down = cross_dot(rows_c, hidden).astype(jnp.bfloat16)
        return grad_acc, (sum_gate, sum_up, sum_down)

    start_acc = jnp.zeros((TOKENS, D), jnp.float32)
    grad_acc, stacked = lax.scan(piece_step, start_acc, jnp.arange(N_EP, dtype=jnp.int32))

    def unstack(parts):
        return parts.transpose(1, 0, 2).reshape(D, N_EP * HID_DEV)

    return (grad_acc.astype(jnp.bfloat16), unstack(stacked[0]), unstack(stacked[1]), unstack(stacked[2]))
```

```python
import jax
import jax.numpy as jnp
from jax import lax
from jax.experimental import pallas as pl
from jax.experimental.pallas import tpu as pltpu
from jax.sharding import PartitionSpec as P

EXPERTS = 8
CAP = 64
TOK = 128
FEAT = 896
HID = 256
MESH = pl.DeviceIdType.MESH

SHIFT = (0, -1, 1, -2, 2, -3, 3, 4)
CHUNKS = ((0, 1), (1, 2), (3, 2), (5, 2), (7, 1))
SEMS = 224

ARRIVAL = (0.0, 10.0, 20.0, 30.0, 36.0)
STEPS = (
    ("zx", -3.0, 0.0),
    ("zc", 0.0, 0.0),
    ("yx", 1.5, 2.5),
    ("yc", 1.6, 5.0),
    ("mx", 2.5, 5.0),
    ("mc", 3.0, 5.5),
    ("sum_far", 5.0, 6.5),
    ("sum_near", 6.5, 8.5),
    ("act", 8.5, 9.5),
    ("spread", 10.5, 10.5),
    ("relay", 12.5, 12.5),
    ("rows", 14.5, 13.5),
    ("pair", 16.5, 14.0),
    ("back", 18.5, 16.5),
    ("wgrad", 19.0, 17.0),
)


def dot_nn(left, right):
    return jnp.dot(left, right, preferred_element_type=jnp.float32)


def dot_nt(left, right):
    return lax.dot_general(
        left, right, (((1,), (1,)), ((), ())), preferred_element_type=jnp.float32
    )


def dot_tn(left, right):
    return lax.dot_general(
        left, right, (((0,), (0,)), ((), ())), preferred_element_type=jnp.float32
    )


def kernel(
    ids_ref, gates_ref, x_ref, c_ref, wg_ref, wu_ref, wd_ref,
    gt_ref, gg_ref, gu_ref, gd_ref,
    meta_own, meta_in, raw, rows, part, far, near, keep, qsend, qrecv, spread,
    term, term_in, tsend, trecv, final, ret, acc, send_sems, recv_sems,
):
    f32, bf16 = jnp.float32, jnp.bfloat16
    ep = lax.axis_index("ep")
    fs = lax.axis_index("fsdp")
    z, yl, co = ep // 4, (ep // 2) % 2, ep % 2
    yh, x = fs // 4, fs % 4
    xp, xm, xo = (x + 1) % 4, (x + 3) % 4, (x + 2) % 4

    def device(plane, ylo, core):
        return (plane * 4 + ylo * 2 + core, fs)

    def ring(step):
        return device((z + step + 8) % 8, yl, co)

    sibling = device(z, yl, 1 - co)
    across = device(z, 1 - yl, co)
    right, left = (ep, yh * 4 + xp), (ep, yh * 4 + xm)
    partner = (ep, (1 - yh) * 4 + x)
    mine, twin = yl * 2 + co, yl * 2 + (1 - co)
    other, other_twin = (1 - yl) * 2 + co, (1 - yl) * 2 + (1 - co)

    places = {}
    started = []

    def copy(name, source, target, where):
        place = places.setdefault(name, len(places))
        return pltpu.make_async_remote_copy(
            src_ref=source,
            dst_ref=target,
            send_sem=send_sems.at[place],
            recv_sem=recv_sems.at[place],
            device_id=where,
            device_id_type=MESH,
        )

    def start(name, source, target, where):
        made = copy(name, source, target, where)
        made.start()
        started.append(made)

    def arrive(name, target):
        copy(name, target, target, sibling).wait_recv()

    barrier = pltpu.get_barrier_semaphore()
    greeted = [ring(step) for step in range(1, 8)] + [sibling, across, right, left, partner]
    for where in greeted:
        pl.semaphore_signal(barrier, inc=1, device_id=where, device_id_type=MESH)
    pl.semaphore_wait(barrier, len(greeted))

    parts = (x_ref, c_ref)
    for p in range(2):
        start(("up", p, 1), parts[p], raw.at[0, p], ring(1))
        start(("down", p, 1), parts[p], raw.at[1, p], ring(-1))

    expert = lax.broadcasted_iota(jnp.int32, (EXPERTS, TOK), 0)
    first, second = ids_ref[0:1, :] == expert, ids_ref[1:2, :] == expert
    member = first | second
    ordered = (
        lax.broadcasted_iota(jnp.int32, (TOK, TOK), 0)
        < lax.broadcasted_iota(jnp.int32, (TOK, TOK), 1)
    )
    before = dot_nn(
        jnp.where(member, 1.0, 0.0).astype(bf16), jnp.where(ordered, 1.0, 0.0).astype(bf16)
    )
    slot = jnp.where(member, before, -1.0)
    gate = jnp.where(first, gates_ref[0:1, :], 0.0) + jnp.where(second, gates_ref[1:2, :], 0.0)
    meta_own[...] = jnp.zeros_like(meta_own)
    for e in range(EXPERTS):
        meta_own[e, 0:1, :] = slot[e : e + 1, :]
        meta_own[e, 1:2, :] = gate[e : e + 1, :]
    for i in range(1, 8):
        plane = (z - SHIFT[i] + 8) % 8
        start(("meta", i), meta_own.at[plane], meta_in.at[i], device(plane, yl, co))
    meta_in[0] = meta_own[z]
    acc[...] = jnp.zeros_like(acc)

    def onehot(slots):
        return slots == lax.broadcasted_iota(jnp.int32, (CAP, TOK), 0).astype(f32)

    def choose(i, p):
        hot = onehot(meta_in[i, 0:1, :])
        block = parts[p][...] if i == 0 else raw[i - 1, p]
        picked = dot_nn(jnp.where(hot, 1.0, 0.0).astype(bf16), block)
        if p == 1:
            weight = jnp.sum(jnp.where(hot, meta_in[i, 1:2, :], 0.0), axis=1, keepdims=True)
            picked = weight * picked
        rows[p, i, mine] = picked.astype(bf16)

    def blocks(k):
        return pl.ds(CHUNKS[k][0], CHUNKS[k][1])

    def each(k):
        return range(CHUNKS[k][0], CHUNKS[k][0] + CHUNKS[k][1])

    def take(k, p):
        if 1 <= k <= 3:
            arrive(("up", p, k), raw.at[2 * k - 2, p])
            if k < 3:
                start(("up", p, k + 1), raw.at[2 * k - 2, p], raw.at[2 * k, p], ring(1))
            elif p == 0:
                start(("far", 0), raw.at[4, 0], raw.at[6, 0], ring(1))
            arrive(("down", p, k), raw.at[2 * k - 1, p])
            if k < 3:
                start(("down", p, k + 1), raw.at[2 * k - 1, p], raw.at[2 * k + 1, p], ring(-1))
            elif p == 1:
                start(("far", 1), raw.at[5, 1], raw.at[6, 1], ring(-1))
        if k == 4:
            arrive(("far", p), raw.at[6, p])
        for i in each(k):
            if p == 0 and i > 0:
                arrive(("meta", i), meta_in.at[i])
            choose(i, p)
        own = rows.at[p, blocks(k), mine]
        start(("across", p, k), own, own, across)
        start(("twin", p, k), own, own, sibling)

    def pass_on(k, p):
        got = rows.at[p, blocks(k), other]
        arrive(("across", p, k), got)
        start(("forward", p, k), got, got, sibling)

    def complete(k, p):
        arrive(("twin", p, k), rows.at[p, blocks(k), twin])
        arrive(("forward", p, k), rows.at[p, blocks(k), other_twin])

    def put(i, at, value):
        part[:, :, i, :, at : at + HID] = value.astype(bf16).reshape(2, 4, 32, HID)

    def multiply_x(k):
        complete(k, 0)
        for i in each(k):
            block = rows[0, i].reshape(4 * CAP, FEAT)
            put(i, 0, dot_nn(block, wg_ref[...]))
            put(i, HID, dot_nn(block, wu_ref[...]))

    def multiply_c(k):
        complete(k, 1)
        for i in each(k):
            put(i, 2 * HID, dot_nn(rows[1, i].reshape(4 * CAP, FEAT), wd_ref[...]))
        at = blocks(k)
        start(("far+", k), part.at[0, xo, at], far.at[0, at], right)
        start(("far-", k), part.at[1, xo, at], far.at[1, at], left)
        start(("own+", k), part.at[1, xp, at], near.at[0, 1, at], right)
        start(("own-", k), part.at[0, xm, at], near.at[1, 0, at], left)

    def sum_far(k):
        at = blocks(k)
        arrive(("far+", k), far.at[0, at])
        part[0, xp, at] = (part[0, xp, at].astype(f32) + far[0, at].astype(f32)).astype(bf16)
        start(("sum+", k), part.at[0, xp, at], near.at[0, 0, at], right)
        arrive(("far-", k), far.at[1, at])
        part[1, xm, at] = (part[1, xm, at].astype(f32) + far[1, at].astype(f32)).astype(bf16)
        start(("sum-", k), part.at[1, xm, at], near.at[1, 1, at], left)

    def sum_near(k):
        at = blocks(k)
        arrive(("own+", k), near.at[0, 1, at])
        arrive(("own-", k), near.at[1, 0, at])
        arrive(("sum+", k), near.at[0, 0, at])
        arrive(("sum-", k), near.at[1, 1, at])

        def total(half):
            return (
                part[half, x, at].astype(f32)
                + near[0, half, at].astype(f32)
                + near[1, half, at].astype(f32)
            )

        qsend[at] = total(1 - yh).astype(bf16)
        start(("q", k), qsend.at[at], qrecv.at[at], partner)
        keep[at] = total(yh)

    def activate(k):
        at = blocks(k)
        arrive(("q", k), qrecv.at[at])
        total = keep[at] + qrecv[at].astype(f32)
        a, u, g = total[:, :, :HID], total[:, :, HID : 2 * HID], total[:, :, 2 * HID :]
        sig = jax.nn.sigmoid(a)
        silu = a * sig
        spread[yh, x, at, :, 0:HID] = (silu * u).astype(bf16)
        spread[yh, x, at, :, HID : 2 * HID] = (g * u * sig * (1.0 + a * (1.0 - sig))).astype(bf16)
        spread[yh, x, at, :, 2 * HID : 3 * HID] = (g * silu).astype(bf16)
        own = spread.at[yh, x, at]
        start(("mate", k), own, own, partner)
        start(("one+", k), own, own, right)
        start(("one-", k), own, own, left)

    def share(k):
        got = spread.at[1 - yh, x, blocks(k)]
        arrive(("mate", k), got)
        start(("two+", k), got, got, right)
        start(("two-", k), got, got, left)

    def relay(k):
        at = blocks(k)
        arrive(("one+", k), spread.at[yh, xm, at])
        arrive(("two+", k), spread.at[1 - yh, xm, at])
        start(("on+", k), spread.at[0, xm, at], spread.at[0, xm, at], right)
        arrive(("one-", k), spread.at[yh, xp, at])
        arrive(("two-", k), spread.at[1 - yh, xp, at])
        start(("on-", k), spread.at[1, xp, at], spread.at[1, xp, at], left)

    def row_terms(k):
        at = blocks(k)
        arrive(("on+", k), spread.at[0, xo, at])
        arrive(("on-", k), spread.at[1, xo, at])
        for i in each(k):
            held = spread[:, :, i].reshape(4 * CAP, 3 * HID)
            value = dot_nt(held[:, HID : 2 * HID], wg_ref[...])
            value = value + dot_nt(held[:, 2 * HID :], wu_ref[...])
            value = value.astype(bf16).reshape(2, 2, CAP, FEAT)
            term[0, i] = value[:, 0]
            term[1, i] = value[:, 1]
        start(("core", k), term.at[1 - co, at], term_in.at[at], sibling)

    def pair(k):
        at = blocks(k)
        arrive(("core", k), term_in.at[at])
        tsend[at] = (
            term[co, at, 1 - yl].astype(f32) + term_in[at, 1 - yl].astype(f32)
        ).astype(bf16)
        start(("ypair", k), tsend.at[at], trecv.at[at], across)

    def back(k):
        at = blocks(k)
        arrive(("ypair", k), trecv.at[at])
        value = (
            term[co, at, yl].astype(f32)
            + term_in[at, yl].astype(f32)
            + trecv[at].astype(f32)
        ).astype(bf16)
        if k == 0:
            ret[0] = value[0]
            return
        final[at] = value
        for i in each(k):
            home = SHIFT.index(-SHIFT[i]) if i < 7 else 7
            start(("ret", home), final.at[i], ret.at[home], ring(SHIFT[i]))

    def weight_grads(k):
        for i in each(k):
            held = spread[:, :, i].reshape(4 * CAP, 3 * HID)
            block = rows[0, i].reshape(4 * CAP, FEAT)
            acc[0] += dot_tn(held[:, HID : 2 * HID], block)
            acc[1] += dot_tn(held[:, 2 * HID :], block)
            acc[2] += dot_tn(held[:, :HID], rows[1, i].reshape(4 * CAP, FEAT))

    run = {
        "zx": lambda k: take(k, 0),
        "zc": lambda k: take(k, 1),
        "yx": lambda k: pass_on(k, 0),
        "yc": lambda k: pass_on(k, 1),
        "mx": multiply_x,
        "mc": multiply_c,
        "sum_far": sum_far,
        "sum_near": sum_near,
        "act": activate,
        "spread": share,
        "relay": relay,
        "rows": row_terms,
        "pair": pair,
        "back": back,
        "wgrad": weight_grads,
    }
    plan = []
    for k in range(len(CHUNKS)):
        for place, (name, fixed, each_block) in enumerate(STEPS):
            plan.append((ARRIVAL[k] + fixed + each_block * CHUNKS[k][1], place, k, name))
    for _, _, k, name in sorted(plan):
        run[name](k)

    gg_ref[...] = acc[0].T.astype(bf16)
    gu_ref[...] = acc[1].T.astype(bf16)
    gd_ref[...] = acc[2].T.astype(bf16)
    hots = []
    for i in range(8):
        if i > 0:
            arrive(("ret", i), ret.at[i])
        slots = meta_own[(z + SHIFT[i] + 8) % 8, 0:1, :]
        hots.append(jnp.where(onehot(slots), 1.0, 0.0).astype(bf16))
    gt_ref[...] = dot_tn(
        jnp.concatenate(hots, axis=0), ret[...].reshape(8 * CAP, FEAT)
    ).astype(bf16)
    for made in started:
        made.wait_send()


def body(tokens, cotangent, route_gates, expert_ids, w_gate, w_up, w_down):
    bf16, f32 = jnp.bfloat16, jnp.float32
    vmem = pl.BlockSpec(memory_space=pltpu.VMEM)
    shape = jax.ShapeDtypeStruct
    return pl.pallas_call(
        kernel,
        out_shape=(
            shape((TOK, FEAT), bf16),
            shape((FEAT, HID), bf16),
            shape((FEAT, HID), bf16),
            shape((FEAT, HID), bf16),
        ),
        in_specs=[vmem] * 7,
        out_specs=(vmem,) * 4,
        scratch_shapes=[
            pltpu.VMEM((EXPERTS, 8, TOK), f32),
            pltpu.VMEM((8, 8, TOK), f32),
            pltpu.VMEM((7, 2, TOK, FEAT), bf16),
            pltpu.VMEM((2, 8, 4, CAP, FEAT), bf16),
            pltpu.VMEM((2, 4, 8, 32, 3 * HID), bf16),
            pltpu.VMEM((2, 8, 32, 3 * HID), bf16),
            pltpu.VMEM((2, 2, 8, 32, 3 * HID), bf16),
            pltpu.VMEM((8, 32, 3 * HID), f32),
            pltpu.VMEM((8, 32, 3 * HID), bf16),
            pltpu.VMEM((8, 32, 3 * HID), bf16),
            pltpu.VMEM((2, 4, 8, 32, 3 * HID), bf16),
            pltpu.VMEM((2, 8, 2, CAP, FEAT), bf16),
            pltpu.VMEM((8, 2, CAP, FEAT), bf16),
            pltpu.VMEM((8, CAP, FEAT), bf16),
            pltpu.VMEM((8, CAP, FEAT), bf16),
            pltpu.VMEM((8, CAP, FEAT), bf16),
            pltpu.VMEM((8, CAP, FEAT), bf16),
            pltpu.VMEM((3, HID, FEAT), f32),
            pltpu.SemaphoreType.DMA((SEMS,)),
            pltpu.SemaphoreType.DMA((SEMS,)),
        ],
        compiler_params=pltpu.CompilerParams(
            collective_id=0, has_side_effects=True, vmem_limit_bytes=60 * 1024 * 1024
        ),
    )(expert_ids.T, route_gates.T, tokens, cotangent, w_gate, w_up, w_down)


def solution(mesh):
    placed = (
        P("ep", "fsdp"),
        P("ep", "fsdp"),
        P("ep", None),
        P("ep", None),
        P("fsdp", "ep"),
        P("fsdp", "ep"),
        P("fsdp", "ep"),
    )
    return jax.shard_map(
        body,
        mesh=mesh,
        in_specs=placed,
        out_specs=(P("ep", "fsdp"), P("fsdp", "ep"), P("fsdp", "ep"), P("fsdp", "ep")),
        check_vma=False,
    )
```

```python
import jax
import jax.numpy as jnp
from jax import lax
from jax.experimental import pallas as pl
from jax.experimental.pallas import tpu as pltpu
from jax.sharding import PartitionSpec as P

EXPERTS = 8
CAP = 64
TOK = 128
FEAT = 896
HID = 256
MESH = pl.DeviceIdType.MESH

SHIFT = (0, -1, 1, -2, 2, -3, 3, 4)
BLOCKS = 8
SEMS = 288

ORDER = (
    0, 8, 1, 2, 10, 17, 9, 16, 18, 4, 26, 34, 3, 42, 25, 33,
    41, 11, 24, 32, 40, 12, 5, 6, 19, 20, 27, 49, 50, 28, 35, 43,
    36, 14, 48, 21, 44, 13, 7, 51, 22, 52, 30, 37, 38, 46, 59, 29,
    15, 54, 23, 45, 67, 56, 62, 60, 53, 31, 39, 47, 75, 61, 70, 55,
    58, 57, 83, 78, 69, 68, 63, 91, 86, 77, 65, 99, 94, 76, 85, 71,
    102, 84, 66, 118, 93, 117, 64, 79, 107, 73, 110, 101, 92, 100, 87, 74,
    109, 81, 95, 72, 108, 82, 103, 89, 97, 80, 90, 111, 114, 98, 88, 112,
    113, 105, 96, 119, 106, 115, 104, 116,
)


def dot_nn(left, right):
    return jnp.dot(left, right, preferred_element_type=jnp.float32)


def dot_nt(left, right):
    return lax.dot_general(
        left, right, (((1,), (1,)), ((), ())), preferred_element_type=jnp.float32
    )


def dot_tn(left, right):
    return lax.dot_general(
        left, right, (((0,), (0,)), ((), ())), preferred_element_type=jnp.float32
    )


def kernel(
    ids_ref, gates_ref, x_ref, c_ref, wg_ref, wu_ref, wd_ref,
    gt_ref, gg_ref, gu_ref, gd_ref,
    meta_own, meta_in, meta_far, raw, rows, far_rows, own, part, far, near,
    keep, qsend, qrecv, spread, term, kept, term_in, tsend, trecv, final, ret, acc,
    send_sems, recv_sems,
):
    f32, bf16 = jnp.float32, jnp.bfloat16
    ep = lax.axis_index("ep")
    fs = lax.axis_index("fsdp")
    z, yl, co = ep // 4, (ep // 2) % 2, ep % 2
    yh, x = fs // 4, fs % 4
    xp, xm, xo = (x + 1) % 4, (x + 3) % 4, (x + 2) % 4

    def device(plane, ylo, core):
        return (plane * 4 + ylo * 2 + core, fs)

    def ring(step):
        return device((z + step + 8) % 8, yl, co)

    sibling = device(z, yl, 1 - co)
    across = device(z, 1 - yl, co)
    right, left = (ep, yh * 4 + xp), (ep, yh * 4 + xm)
    partner = (ep, (1 - yh) * 4 + x)
    mine, twin = yl * 2 + co, yl * 2 + (1 - co)
    other, other_twin = (1 - yl) * 2 + co, (1 - yl) * 2 + (1 - co)

    places = {}
    started = []

    def copy(name, source, target, where):
        place = places.setdefault(name, len(places))
        return pltpu.make_async_remote_copy(
            src_ref=source,
            dst_ref=target,
            send_sem=send_sems.at[place],
            recv_sem=recv_sems.at[place],
            device_id=where,
            device_id_type=MESH,
        )

    def start(name, source, target, where):
        made = copy(name, source, target, where)
        made.start()
        started.append(made)

    def arrive(name, target):
        copy(name, target, target, sibling).wait_recv()

    barrier = pltpu.get_barrier_semaphore()
    greeted = [ring(step) for step in range(1, 8)] + [sibling, across, right, left, partner]
    for where in greeted:
        pl.semaphore_signal(barrier, inc=1, device_id=where, device_id_type=MESH)
    pl.semaphore_wait(barrier, len(greeted))

    parts = (x_ref, c_ref)
    for p in range(2):
        start(("up", p, 1), parts[p], raw.at[0, p], ring(1))
        start(("down", p, 2), parts[p], raw.at[1, p], ring(-1))

    expert = lax.broadcasted_iota(jnp.int32, (EXPERTS, TOK), 0)
    first, second = ids_ref[0:1, :] == expert, ids_ref[1:2, :] == expert
    member = first | second
    ordered = (
        lax.broadcasted_iota(jnp.int32, (TOK, TOK), 0)
        < lax.broadcasted_iota(jnp.int32, (TOK, TOK), 1)
    )
    before = dot_nn(
        jnp.where(member, 1.0, 0.0).astype(bf16), jnp.where(ordered, 1.0, 0.0).astype(bf16)
    )
    slot = jnp.where(member, before, -1.0)
    gate = jnp.where(first, gates_ref[0:1, :], 0.0) + jnp.where(second, gates_ref[1:2, :], 0.0)
    meta_own[...] = jnp.zeros_like(meta_own)
    for e in range(EXPERTS):
        meta_own[e, 0:1, :] = slot[e : e + 1, :]
        meta_own[e, 1:2, :] = gate[e : e + 1, :]
    for i in range(1, 7):
        plane = (z - SHIFT[i] + 8) % 8
        start(("meta", i), meta_own.at[plane], meta_in.at[i], device(plane, yl, co))
    facing = meta_own.at[(z + 4) % 8]
    start(("meta", 8), facing, meta_far.at[0], ring(3))
    start(("meta", 9), facing, meta_far.at[1], ring(-3))
    meta_in[0] = meta_own[z]
    acc[...] = jnp.zeros_like(acc)

    def onehot(slots):
        return slots == lax.broadcasted_iota(jnp.int32, (CAP, TOK), 0).astype(f32)

    def choose(block, meta, p):
        hot = onehot(meta[0:1, :])
        picked = dot_nn(jnp.where(hot, 1.0, 0.0).astype(bf16), block)
        if p == 1:
            weight = jnp.sum(jnp.where(hot, meta[1:2, :], 0.0), axis=1, keepdims=True)
            picked = weight * picked
        return picked.astype(bf16)

    def take(i, p):
        if 1 <= i <= 6:
            name, away = ("up", 1) if i % 2 else ("down", -1)
            got = raw.at[i - 1, p]
            arrive((name, p, i), got)
            if i < 5:
                start((name, p, i + 2), got, raw.at[i + 1, p], ring(away))
            elif p == i - 5:
                arrive(("meta", 8 + p), meta_far.at[p])
                far_rows[p] = choose(raw[i - 1, p], meta_far[p], p)
                start(("last", p), far_rows.at[p], rows.at[p, 7, mine], ring(away))
        if i == 7:
            arrive(("last", p), rows.at[p, 7, mine])
        else:
            if p == 0 and i > 0:
                arrive(("meta", i), meta_in.at[i])
            block = parts[p][...] if i == 0 else raw[i - 1, p]
            rows[p, i, mine] = choose(block, meta_in[i], p)
        chosen = rows.at[p, i, mine]
        start(("across", p, i), chosen, chosen, across)
        start(("twin", p, i), chosen, chosen, sibling)

    def pass_on(i, p):
        got = rows.at[p, i, other]
        arrive(("across", p, i), got)
        start(("forward", p, i), got, got, sibling)

    def complete(i, p):
        arrive(("twin", p, i), rows.at[p, i, twin])
        arrive(("forward", p, i), rows.at[p, i, other_twin])

    def put(i, at, value):
        value = value.reshape(2, 4, 32, HID)
        own[:, :, i, :, at : at + HID] = value
        part[:, :, i, :, at : at + HID] = value.astype(bf16)

    def multiply_x(i):
        complete(i, 0)
        block = rows[0, i].reshape(4 * CAP, FEAT)
        put(i, 0, dot_nn(block, wg_ref[...]))
        put(i, HID, dot_nn(block, wu_ref[...]))

    def multiply_c(i):
        complete(i, 1)
        put(i, 2 * HID, dot_nn(rows[1, i].reshape(4 * CAP, FEAT), wd_ref[...]))
        start(("far+", i), part.at[0, xo, i], far.at[0, i], right)
        start(("far-", i), part.at[1, xo, i], far.at[1, i], left)
        start(("own+", i), part.at[1, xp, i], near.at[0, 1, i], right)
        start(("own-", i), part.at[0, xm, i], near.at[1, 0, i], left)

    def sum_far(i):
        arrive(("far+", i), far.at[0, i])
        part[0, xp, i] = (own[0, xp, i] + far[0, i].astype(f32)).astype(bf16)
        start(("sum+", i), part.at[0, xp, i], near.at[0, 0, i], right)
        arrive(("far-", i), far.at[1, i])
        part[1, xm, i] = (own[1, xm, i] + far[1, i].astype(f32)).astype(bf16)
        start(("sum-", i), part.at[1, xm, i], near.at[1, 1, i], left)

    def sum_near(i):
        arrive(("own+", i), near.at[0, 1, i])
        arrive(("own-", i), near.at[1, 0, i])
        arrive(("sum+", i), near.at[0, 0, i])
        arrive(("sum-", i), near.at[1, 1, i])

        def total(half):
            return own[half, x, i] + near[0, half, i].astype(f32) + near[1, half, i].astype(f32)

        qsend[i] = total(1 - yh).astype(bf16)
        start(("q", i), qsend.at[i], qrecv.at[i], partner)
        keep[i] = total(yh)

    def activate(i):
        arrive(("q", i), qrecv.at[i])
        total = keep[i] + qrecv[i].astype(f32)
        a, u, g = total[:, :HID], total[:, HID : 2 * HID], total[:, 2 * HID :]
        sig = jax.nn.sigmoid(a)
        silu = a * sig
        spread[yh, x, i, :, 0:HID] = (silu * u).astype(bf16)
        spread[yh, x, i, :, HID : 2 * HID] = (g * u * sig * (1.0 + a * (1.0 - sig))).astype(bf16)
        spread[yh, x, i, :, 2 * HID : 3 * HID] = (g * silu).astype(bf16)
        made = spread.at[yh, x, i]
        start(("mate", i), made, made, partner)
        start(("one+", i), made, made, right)
        start(("one-", i), made, made, left)

    def share(i):
        got = spread.at[1 - yh, x, i]
        arrive(("mate", i), got)
        start(("two+", i), got, got, right)
        start(("two-", i), got, got, left)

    def relay(i):
        arrive(("one+", i), spread.at[yh, xm, i])
        arrive(("two+", i), spread.at[1 - yh, xm, i])
        start(("on+", i), spread.at[0, xm, i], spread.at[0, xm, i], right)
        arrive(("one-", i), spread.at[yh, xp, i])
        arrive(("two-", i), spread.at[1 - yh, xp, i])
        start(("on-", i), spread.at[1, xp, i], spread.at[1, xp, i], left)

    def row_terms(i):
        arrive(("on+", i), spread.at[0, xo, i])
        arrive(("on-", i), spread.at[1, xo, i])

        def product(core):
            held = spread[:, pl.ds(2 * core, 2), i].reshape(2 * CAP, 3 * HID)
            value = dot_nt(held[:, HID : 2 * HID], wg_ref[...])
            value = value + dot_nt(held[:, 2 * HID :], wu_ref[...])
            return value.reshape(2, CAP, FEAT)

        term[i] = product(1 - co).astype(bf16)
        start(("core", i), term.at[i], term_in.at[i], sibling)
        kept[i] = product(co)

    def pair(i):
        arrive(("core", i), term_in.at[i])
        tsend[i] = (kept[i, 1 - yl] + term_in[i, 1 - yl].astype(f32)).astype(bf16)
        start(("ypair", i), tsend.at[i], trecv.at[i], across)

    def back(i):
        arrive(("ypair", i), trecv.at[i])
        value = kept[i, yl] + term_in[i, yl].astype(f32) + trecv[i].astype(f32)
        if i == 0:
            ret[0] = value.astype(bf16)
            return
        final[i] = value.astype(bf16)
        home = SHIFT.index(-SHIFT[i]) if i < 7 else 7
        start(("ret", home), final.at[i], ret.at[home], ring(SHIFT[i]))

    def weight_grads(i):
        held = spread[:, :, i].reshape(4 * CAP, 3 * HID)
        block = rows[0, i].reshape(4 * CAP, FEAT)
        acc[0] += dot_tn(held[:, HID : 2 * HID], block)
        acc[1] += dot_tn(held[:, 2 * HID :], block)
        acc[2] += dot_tn(held[:, :HID], rows[1, i].reshape(4 * CAP, FEAT))

    run = (
        lambda i: take(i, 0),
        lambda i: take(i, 1),
        lambda i: pass_on(i, 0),
        lambda i: pass_on(i, 1),
        multiply_x,
        multiply_c,
        sum_far,
        sum_near,
        activate,
        share,
        relay,
        row_terms,
        pair,
        back,
        weight_grads,
    )
    for item in ORDER:
        run[item // BLOCKS](item % BLOCKS)

    gg_ref[...] = acc[0].T.astype(bf16)
    gu_ref[...] = acc[1].T.astype(bf16)
    gd_ref[...] = acc[2].T.astype(bf16)
    hots = []
    for i in range(8):
        if i > 0:
            arrive(("ret", i), ret.at[i])
        slots = meta_own[(z + SHIFT[i] + 8) % 8, 0:1, :]
        hots.append(jnp.where(onehot(slots), 1.0, 0.0).astype(bf16))
    gt_ref[...] = dot_tn(
        jnp.concatenate(hots, axis=0), ret[...].reshape(8 * CAP, FEAT)
    ).astype(bf16)
    for made in started:
        made.wait_send()


def body(tokens, cotangent, route_gates, expert_ids, w_gate, w_up, w_down):
    bf16, f32 = jnp.bfloat16, jnp.float32
    vmem = pl.BlockSpec(memory_space=pltpu.VMEM)
    shape = jax.ShapeDtypeStruct
    return pl.pallas_call(
        kernel,
        out_shape=(
            shape((TOK, FEAT), bf16),
            shape((FEAT, HID), bf16),
            shape((FEAT, HID), bf16),
            shape((FEAT, HID), bf16),
        ),
        in_specs=[vmem] * 7,
        out_specs=(vmem,) * 4,
        scratch_shapes=[
            pltpu.VMEM((EXPERTS, 8, TOK), f32),
            pltpu.VMEM((8, 8, TOK), f32),
            pltpu.VMEM((2, 8, TOK), f32),
            pltpu.VMEM((6, 2, TOK, FEAT), bf16),
            pltpu.VMEM((2, 8, 4, CAP, FEAT), bf16),
            pltpu.VMEM((2, CAP, FEAT), bf16),
            pltpu.VMEM((2, 4, 8, 32, 3 * HID), f32),
            pltpu.VMEM((2, 4, 8, 32, 3 * HID), bf16),
            pltpu.VMEM((2, 8, 32, 3 * HID), bf16),
            pltpu.VMEM((2, 2, 8, 32, 3 * HID), bf16),
            pltpu.VMEM((8, 32, 3 * HID), f32),
            pltpu.VMEM((8, 32, 3 * HID), bf16),
            pltpu.VMEM((8, 32, 3 * HID), bf16),
            pltpu.VMEM((2, 4, 8, 32, 3 * HID), bf16),
            pltpu.VMEM((8, 2, CAP, FEAT), bf16),
            pltpu.VMEM((8, 2, CAP, FEAT), f32),
            pltpu.VMEM((8, 2, CAP, FEAT), bf16),
            pltpu.VMEM((8, CAP, FEAT), bf16),
            pltpu.VMEM((8, CAP, FEAT), bf16),
            pltpu.VMEM((8, CAP, FEAT), bf16),
            pltpu.VMEM((8, CAP, FEAT), bf16),
            pltpu.VMEM((3, HID, FEAT), f32),
            pltpu.SemaphoreType.DMA((SEMS,)),
            pltpu.SemaphoreType.DMA((SEMS,)),
        ],
        compiler_params=pltpu.CompilerParams(
            collective_id=0, has_side_effects=True, vmem_limit_bytes=60 * 1024 * 1024
        ),
    )(expert_ids.T, route_gates.T, tokens, cotangent, w_gate, w_up, w_down)


def solution(mesh):
    placed = (
        P("ep", "fsdp"),
        P("ep", "fsdp"),
        P("ep", None),
        P("ep", None),
        P("fsdp", "ep"),
        P("fsdp", "ep"),
        P("fsdp", "ep"),
    )
    return jax.shard_map(
        body,
        mesh=mesh,
        in_specs=placed,
        out_specs=(P("ep", "fsdp"), P("fsdp", "ep"), P("fsdp", "ep"), P("fsdp", "ep")),
        check_vma=False,
    )
```

```python
import jax
import jax.numpy as jnp
from jax import lax
from jax.experimental import pallas as pl
from jax.experimental.pallas import tpu as pltpu
from jax.sharding import PartitionSpec as P

EXPERTS = 8
CAP = 64
TOK = 128
FEAT = 896
HID = 256
MESH = pl.DeviceIdType.MESH

SHIFT = (0, -1, 1, -2, 2, -3, 3, 4)
BLOCKS = 8
SEMS = 288

ORDER = (
    0, 8, 1, 2, 16, 10, 9, 4, 3, 24, 17, 32, 40, 11, 12, 26,
    25, 33, 41, 18, 48, 6, 5, 34, 42, 19, 27, 35, 43, 20, 49, 13,
    28, 14, 36, 44, 50, 51, 21, 22, 29, 7, 15, 38, 52, 37, 45, 30,
    58, 46, 60, 53, 23, 31, 59, 54, 39, 47, 61, 68, 62, 55, 67, 69,
    76, 70, 63, 57, 77, 56, 84, 78, 85, 71, 75, 66, 92, 86, 65, 100,
    93, 83, 101, 79, 74, 73, 94, 118, 64, 116, 91, 108, 102, 87, 109, 82,
    99, 81, 117, 72, 95, 110, 90, 119, 103, 89, 107, 113, 114, 98, 80, 97,
    111, 88, 96, 105, 106, 104, 115, 112,
)


def dot_nn(left, right):
    return jnp.dot(left, right, preferred_element_type=jnp.float32)


def dot_nt(left, right):
    return lax.dot_general(
        left, right, (((1,), (1,)), ((), ())), preferred_element_type=jnp.float32
    )


def dot_tn(left, right):
    return lax.dot_general(
        left, right, (((0,), (0,)), ((), ())), preferred_element_type=jnp.float32
    )


def kernel(
    ids_ref, gates_ref, x_in, c_in, wg_in, wu_in, wd_in,
    gt_out, gg_out, gu_out, gd_out,
    x_ref, c_ref, wg_ref, wu_ref, wd_ref, gt_ref, wgrads,
    meta_own, meta_in, meta_far, raw, rows, far_rows, own, part, far, near,
    keep, qsend, qrecv, spread, term, kept, term_in, tsend, trecv, final, ret, acc,
    send_sems, recv_sems, load_sems, store_sems,
):
    f32, bf16 = jnp.float32, jnp.bfloat16
    ep = lax.axis_index("ep")
    fs = lax.axis_index("fsdp")
    z, yl, co = ep // 4, (ep // 2) % 2, ep % 2
    yh, x = fs // 4, fs % 4
    xp, xm, xo = (x + 1) % 4, (x + 3) % 4, (x + 2) % 4

    def device(plane, ylo, core):
        return (plane * 4 + ylo * 2 + core, fs)

    def ring(step):
        return device((z + step + 8) % 8, yl, co)

    sibling = device(z, yl, 1 - co)
    across = device(z, 1 - yl, co)
    right, left = (ep, yh * 4 + xp), (ep, yh * 4 + xm)
    partner = (ep, (1 - yh) * 4 + x)
    mine, twin = yl * 2 + co, yl * 2 + (1 - co)
    other, other_twin = (1 - yl) * 2 + co, (1 - yl) * 2 + (1 - co)

    places = {}
    started = []

    def copy(name, source, target, where):
        place = places.setdefault(name, len(places))
        return pltpu.make_async_remote_copy(
            src_ref=source,
            dst_ref=target,
            send_sem=send_sems.at[place],
            recv_sem=recv_sems.at[place],
            device_id=where,
            device_id_type=MESH,
        )

    def start(name, source, target, where):
        made = copy(name, source, target, where)
        made.start()
        started.append(made)

    def arrive(name, target):
        copy(name, target, target, sibling).wait_recv()

    barrier = pltpu.get_barrier_semaphore()
    greeted = [ring(step) for step in range(1, 8)] + [sibling, across, right, left, partner]
    for where in greeted:
        pl.semaphore_signal(barrier, inc=1, device_id=where, device_id_type=MESH)

    loads = [
        pltpu.make_async_copy(source, target, load_sems.at[place])
        for place, (source, target) in enumerate(
            ((x_in, x_ref), (c_in, c_ref), (wg_in, wg_ref), (wu_in, wu_ref), (wd_in, wd_ref))
        )
    ]
    for load in loads:
        load.start()
    parts = (x_ref, c_ref)

    expert = lax.broadcasted_iota(jnp.int32, (EXPERTS, TOK), 0)
    first, second = ids_ref[0:1, :] == expert, ids_ref[1:2, :] == expert
    member = first | second
    ordered = (
        lax.broadcasted_iota(jnp.int32, (TOK, TOK), 0)
        < lax.broadcasted_iota(jnp.int32, (TOK, TOK), 1)
    )
    before = dot_nn(
        jnp.where(member, 1.0, 0.0).astype(bf16), jnp.where(ordered, 1.0, 0.0).astype(bf16)
    )
    slot = jnp.where(member, before, -1.0)
    gate = jnp.where(first, gates_ref[0:1, :], 0.0) + jnp.where(second, gates_ref[1:2, :], 0.0)
    meta_own[...] = jnp.zeros_like(meta_own)
    for e in range(EXPERTS):
        meta_own[e, 0:1, :] = slot[e : e + 1, :]
        meta_own[e, 1:2, :] = gate[e : e + 1, :]
    meta_in[0] = meta_own[z]
    acc[...] = jnp.zeros_like(acc)

    pl.semaphore_wait(barrier, len(greeted))
    for p in range(2):
        loads[p].wait()
        start(("up", p, 1), parts[p], raw.at[0, p], ring(1))
        start(("down", p, 2), parts[p], raw.at[1, p], ring(-1))
    for i in range(1, 7):
        plane = (z - SHIFT[i] + 8) % 8
        start(("meta", i), meta_own.at[plane], meta_in.at[i], device(plane, yl, co))
    facing = meta_own.at[(z + 4) % 8]
    start(("meta", 8), facing, meta_far.at[0], ring(3))
    start(("meta", 9), facing, meta_far.at[1], ring(-3))

    def onehot(slots):
        return slots == lax.broadcasted_iota(jnp.int32, (CAP, TOK), 0).astype(f32)

    def choose(block, meta, p):
        hot = onehot(meta[0:1, :])
        picked = dot_nn(jnp.where(hot, 1.0, 0.0).astype(bf16), block)
        if p == 1:
            weight = jnp.sum(jnp.where(hot, meta[1:2, :], 0.0), axis=1, keepdims=True)
            picked = weight * picked
        return picked.astype(bf16)

    def take(i, p):
        if 1 <= i <= 6:
            name, away = ("up", 1) if i % 2 else ("down", -1)
            got = raw.at[i - 1, p]
            arrive((name, p, i), got)
            if i < 5:
                start((name, p, i + 2), got, raw.at[i + 1, p], ring(away))
            elif p == i - 5:
                arrive(("meta", 8 + p), meta_far.at[p])
                far_rows[p] = choose(raw[i - 1, p], meta_far[p], p)
                start(("last", p), far_rows.at[p], rows.at[p, 7, mine], ring(away))
        if i == 7:
            arrive(("last", p), rows.at[p, 7, mine])
        else:
            if p == 0 and i > 0:
                arrive(("meta", i), meta_in.at[i])
            block = parts[p][...] if i == 0 else raw[i - 1, p]
            rows[p, i, mine] = choose(block, meta_in[i], p)
        chosen = rows.at[p, i, mine]
        start(("across", p, i), chosen, chosen, across)
        start(("twin", p, i), chosen, chosen, sibling)

    def pass_on(i, p):
        got = rows.at[p, i, other]
        arrive(("across", p, i), got)
        start(("forward", p, i), got, got, sibling)

    def complete(i, p):
        arrive(("twin", p, i), rows.at[p, i, twin])
        arrive(("forward", p, i), rows.at[p, i, other_twin])

    def put(i, at, value):
        value = value.reshape(2, 4, 32, HID)
        own[:, :, i, :, at : at + HID] = value
        part[:, :, i, :, at : at + HID] = value.astype(bf16)

    def multiply_x(i):
        complete(i, 0)
        block = rows[0, i].reshape(4 * CAP, FEAT)
        put(i, 0, dot_nn(block, wg_ref[...]))
        put(i, HID, dot_nn(block, wu_ref[...]))

    def multiply_c(i):
        complete(i, 1)
        put(i, 2 * HID, dot_nn(rows[1, i].reshape(4 * CAP, FEAT), wd_ref[...]))
        start(("far+", i), part.at[0, xo, i], far.at[0, i], right)
        start(("far-", i), part.at[1, xo, i], far.at[1, i], left)
        start(("own+", i), part.at[1, xp, i], near.at[0, 1, i], right)
        start(("own-", i), part.at[0, xm, i], near.at[1, 0, i], left)

    def sum_far(i):
        arrive(("far+", i), far.at[0, i])
        part[0, xp, i] = (own[0, xp, i] + far[0, i].astype(f32)).astype(bf16)
        start(("sum+", i), part.at[0, xp, i], near.at[0, 0, i], right)
        arrive(("far-", i), far.at[1, i])
        part[1, xm, i] = (own[1, xm, i] + far[1, i].astype(f32)).astype(bf16)
        start(("sum-", i), part.at[1, xm, i], near.at[1, 1, i], left)

    def sum_near(i):
        arrive(("own+", i), near.at[0, 1, i])
        arrive(("own-", i), near.at[1, 0, i])
        arrive(("sum+", i), near.at[0, 0, i])
        arrive(("sum-", i), near.at[1, 1, i])

        def total(half):
            return own[half, x, i] + near[0, half, i].astype(f32) + near[1, half, i].astype(f32)

        qsend[i] = total(1 - yh).astype(bf16)
        start(("q", i), qsend.at[i], qrecv.at[i], partner)
        keep[i] = total(yh)

    def activate(i):
        arrive(("q", i), qrecv.at[i])
        total = keep[i] + qrecv[i].astype(f32)
        a, u, g = total[:, :HID], total[:, HID : 2 * HID], total[:, 2 * HID :]
        sig = jax.nn.sigmoid(a)
        silu = a * sig
        spread[yh, x, i, :, 0:HID] = (silu * u).astype(bf16)
        spread[yh, x, i, :, HID : 2 * HID] = (g * u * sig * (1.0 + a * (1.0 - sig))).astype(bf16)
        spread[yh, x, i, :, 2 * HID : 3 * HID] = (g * silu).astype(bf16)
        made = spread.at[yh, x, i]
        start(("mate", i), made, made, partner)
        start(("one+", i), made, made, right)
        start(("one-", i), made, made, left)

    def share(i):
        got = spread.at[1 - yh, x, i]
        arrive(("mate", i), got)
        start(("two+", i), got, got, right)
        start(("two-", i), got, got, left)

    def relay(i):
        arrive(("one+", i), spread.at[yh, xm, i])
        arrive(("two+", i), spread.at[1 - yh, xm, i])
        start(("on+", i), spread.at[0, xm, i], spread.at[0, xm, i], right)
        arrive(("one-", i), spread.at[yh, xp, i])
        arrive(("two-", i), spread.at[1 - yh, xp, i])
        start(("on-", i), spread.at[1, xp, i], spread.at[1, xp, i], left)

    def row_terms(i):
        arrive(("on+", i), spread.at[0, xo, i])
        arrive(("on-", i), spread.at[1, xo, i])

        def product(core):
            held = spread[:, pl.ds(2 * core, 2), i].reshape(2 * CAP, 3 * HID)
            value = dot_nt(held[:, HID : 2 * HID], wg_ref[...])
            value = value + dot_nt(held[:, 2 * HID :], wu_ref[...])
            return value.reshape(2, CAP, FEAT)

        term[i] = product(1 - co).astype(bf16)
        start(("core", i), term.at[i], term_in.at[i], sibling)
        kept[i] = product(co)

    def pair(i):
        arrive(("core", i), term_in.at[i])
        tsend[i] = (kept[i, 1 - yl] + term_in[i, 1 - yl].astype(f32)).astype(bf16)
        start(("ypair", i), tsend.at[i], trecv.at[i], across)

    def back(i):
        arrive(("ypair", i), trecv.at[i])
        value = kept[i, yl] + term_in[i, yl].astype(f32) + trecv[i].astype(f32)
        if i == 0:
            ret[0] = value.astype(bf16)
            return
        final[i] = value.astype(bf16)
        home = SHIFT.index(-SHIFT[i]) if i < 7 else 7
        start(("ret", home), final.at[i], ret.at[home], ring(SHIFT[i]))

    def weight_grads(i):
        held = spread[:, :, i].reshape(4 * CAP, 3 * HID)
        block = rows[0, i].reshape(4 * CAP, FEAT)
        acc[0] += dot_tn(held[:, HID : 2 * HID], block)
        acc[1] += dot_tn(held[:, 2 * HID :], block)
        acc[2] += dot_tn(held[:, :HID], rows[1, i].reshape(4 * CAP, FEAT))

    run = (
        lambda i: take(i, 0),
        lambda i: take(i, 1),
        lambda i: pass_on(i, 0),
        lambda i: pass_on(i, 1),
        multiply_x,
        multiply_c,
        sum_far,
        sum_near,
        activate,
        share,
        relay,
        row_terms,
        pair,
        back,
        weight_grads,
    )
    loaded = False
    for item in ORDER:
        if run[item // BLOCKS] is multiply_x and not loaded:
            for load in loads[2:]:
                load.wait()
            loaded = True
        run[item // BLOCKS](item % BLOCKS)

    stores = []
    for place, target in enumerate((gg_out, gu_out, gd_out)):
        wgrads[place] = acc[place].T.astype(bf16)
        stores.append(pltpu.make_async_copy(wgrads.at[place], target, store_sems.at[place]))
        stores[-1].start()
    hots = []
    for i in range(8):
        slots = meta_own[(z + SHIFT[i] + 8) % 8, 0:1, :]
        hots.append(jnp.where(onehot(slots), 1.0, 0.0).astype(bf16))
    hots = jnp.concatenate(hots, axis=0)
    for made in started:
        made.wait_send()
    for i in range(1, 8):
        arrive(("ret", i), ret.at[i])
    gt_ref[...] = dot_tn(hots, ret[...].reshape(8 * CAP, FEAT)).astype(bf16)
    stores.append(pltpu.make_async_copy(gt_ref, gt_out, store_sems.at[3]))
    stores[-1].start()
    for store in stores:
        store.wait()


def hand_on(*refs):
    for source, target in zip(refs[:4], refs[4:]):
        target[...] = source[...]


def body(tokens, cotangent, route_gates, expert_ids, w_gate, w_up, w_down):
    bf16, f32 = jnp.bfloat16, jnp.float32
    vmem = pl.BlockSpec(memory_space=pltpu.VMEM)
    anywhere = pl.BlockSpec(memory_space=pl.ANY)
    shape = jax.ShapeDtypeStruct
    outs = (shape((TOK, FEAT), bf16),) + (shape((FEAT, HID), bf16),) * 3
    results = pl.pallas_call(
        kernel,
        out_shape=outs,
        in_specs=[vmem] * 2 + [anywhere] * 5,
        out_specs=(anywhere,) * 4,
        scratch_shapes=[
            pltpu.VMEM((TOK, FEAT), bf16),
            pltpu.VMEM((TOK, FEAT), bf16),
            pltpu.VMEM((FEAT, HID), bf16),
            pltpu.VMEM((FEAT, HID), bf16),
            pltpu.VMEM((FEAT, HID), bf16),
            pltpu.VMEM((TOK, FEAT), bf16),
            pltpu.VMEM((3, FEAT, HID), bf16),
            pltpu.VMEM((EXPERTS, 8, TOK), f32),
            pltpu.VMEM((8, 8, TOK), f32),
            pltpu.VMEM((2, 8, TOK), f32),
            pltpu.VMEM((6, 2, TOK, FEAT), bf16),
            pltpu.VMEM((2, 8, 4, CAP, FEAT), bf16),
            pltpu.VMEM((2, CAP, FEAT), bf16),
            pltpu.VMEM((2, 4, 8, 32, 3 * HID), f32),
            pltpu.VMEM((2, 4, 8, 32, 3 * HID), bf16),
            pltpu.VMEM((2, 8, 32, 3 * HID), bf16),
            pltpu.VMEM((2, 2, 8, 32, 3 * HID), bf16),
            pltpu.VMEM((8, 32, 3 * HID), f32),
            pltpu.VMEM((8, 32, 3 * HID), bf16),
            pltpu.VMEM((8, 32, 3 * HID), bf16),
            pltpu.VMEM((2, 4, 8, 32, 3 * HID), bf16),
            pltpu.VMEM((8, 2, CAP, FEAT), bf16),
            pltpu.VMEM((8, 2, CAP, FEAT), f32),
            pltpu.VMEM((8, 2, CAP, FEAT), bf16),
            pltpu.VMEM((8, CAP, FEAT), bf16),
            pltpu.VMEM((8, CAP, FEAT), bf16),
            pltpu.VMEM((8, CAP, FEAT), bf16),
            pltpu.VMEM((8, CAP, FEAT), bf16),
            pltpu.VMEM((3, HID, FEAT), f32),
            pltpu.SemaphoreType.DMA((SEMS,)),
            pltpu.SemaphoreType.DMA((SEMS,)),
            pltpu.SemaphoreType.DMA((5,)),
            pltpu.SemaphoreType.DMA((4,)),
        ],
        compiler_params=pltpu.CompilerParams(
            collective_id=0, has_side_effects=True, vmem_limit_bytes=60 * 1024 * 1024
        ),
    )(expert_ids.T, route_gates.T, tokens, cotangent, w_gate, w_up, w_down)
    return pl.pallas_call(
        hand_on,
        out_shape=outs,
        in_specs=[vmem] * 4,
        out_specs=(vmem,) * 4,
    )(*results)


def solution(mesh):
    placed = (
        P("ep", "fsdp"),
        P("ep", "fsdp"),
        P("ep", None),
        P("ep", None),
        P("fsdp", "ep"),
        P("fsdp", "ep"),
        P("fsdp", "ep"),
    )
    return jax.shard_map(
        body,
        mesh=mesh,
        in_specs=placed,
        out_specs=(P("ep", "fsdp"), P("fsdp", "ep"), P("fsdp", "ep"), P("fsdp", "ep")),
        check_vma=False,
    )
```

```python
import jax
import jax.numpy as jnp
from jax import lax
from jax.experimental import pallas as pl
from jax.experimental.pallas import tpu as pltpu
from jax.sharding import PartitionSpec as P

EXPERTS = 8
CAP = 64
TOK = 128
FEAT = 896
HID = 256
MESH = pl.DeviceIdType.MESH

SHIFT = (0, -1, 1, -2, 2, -3, 3, 4)
BLOCKS = 8
SEMS = 288

ORDER = (
    0, 8, 1, 16, 2, 24, 9, 10, 32, 40, 18, 3, 4, 25, 34, 26,
    17, 12, 42, 11, 33, 41, 6, 5, 20, 28, 19, 50, 36, 44, 27, 14,
    35, 43, 13, 22, 48, 49, 52, 21, 7, 15, 30, 51, 38, 46, 29, 37,
    45, 23, 59, 60, 54, 39, 31, 58, 53, 47, 62, 67, 61, 55, 68, 75,
    56, 70, 63, 76, 69, 57, 83, 78, 91, 84, 77, 71, 92, 86, 65, 94,
    85, 79, 99, 66, 93, 100, 73, 64, 102, 87, 111, 74, 101, 95, 81, 72,
    89, 82, 106, 103, 90, 80, 107, 88, 108, 97, 110, 98, 96, 109, 105, 104,
)


def dot_nn(left, right):
    return jnp.dot(left, right, preferred_element_type=jnp.float32)


def dot_nt(left, right):
    return lax.dot_general(
        left, right, (((1,), (1,)), ((), ())), preferred_element_type=jnp.float32
    )


def dot_tn(left, right):
    return lax.dot_general(
        left, right, (((0,), (0,)), ((), ())), preferred_element_type=jnp.float32
    )


def kernel(
    ids_ref, gates_ref, x_in, c_in, wg_in, wu_in, wd_in,
    gt_out, gg_out, gu_out, gd_out,
    x_ref, c_ref, wg_ref, wu_ref, wd_ref, gt_ref, wgrads,
    meta_own, meta_in, meta_far, raw, rows, far_rows, own, part, far, near,
    keep, qsend, qrecv, spread, term, kept, term_in, tsend, trecv, final, ret, acc,
    send_sems, recv_sems, load_sems, store_sems,
):
    f32, bf16 = jnp.float32, jnp.bfloat16
    ep = lax.axis_index("ep")
    fs = lax.axis_index("fsdp")
    z, yl, co = ep // 4, (ep // 2) % 2, ep % 2
    yh, x = fs // 4, fs % 4
    xp, xm, xo = (x + 1) % 4, (x + 3) % 4, (x + 2) % 4

    def device(plane, ylo, core):
        return (plane * 4 + ylo * 2 + core, fs)

    def ring(step):
        return device((z + step + 8) % 8, yl, co)

    sibling = device(z, yl, 1 - co)
    across = device(z, 1 - yl, co)
    right, left = (ep, yh * 4 + xp), (ep, yh * 4 + xm)
    partner = (ep, (1 - yh) * 4 + x)
    mine, twin = yl * 2 + co, yl * 2 + (1 - co)
    other, other_twin = (1 - yl) * 2 + co, (1 - yl) * 2 + (1 - co)

    places = {}
    started = []

    def copy(name, source, target, where):
        place = places.setdefault(name, len(places))
        return pltpu.make_async_remote_copy(
            src_ref=source,
            dst_ref=target,
            send_sem=send_sems.at[place],
            recv_sem=recv_sems.at[place],
            device_id=where,
            device_id_type=MESH,
        )

    def start(name, source, target, where):
        made = copy(name, source, target, where)
        made.start()
        started.append(made)

    def arrive(name, target):
        copy(name, target, target, sibling).wait_recv()

    barrier = pltpu.get_barrier_semaphore()
    greeted = [ring(step) for step in range(1, 8)] + [sibling, across, right, left, partner]
    for where in greeted:
        pl.semaphore_signal(barrier, inc=1, device_id=where, device_id_type=MESH)

    loads = [
        pltpu.make_async_copy(source, target, load_sems.at[place])
        for place, (source, target) in enumerate(
            ((x_in, x_ref), (c_in, c_ref), (wg_in, wg_ref), (wu_in, wu_ref), (wd_in, wd_ref))
        )
    ]
    for load in loads:
        load.start()
    parts = (x_ref, c_ref)

    expert = lax.broadcasted_iota(jnp.int32, (EXPERTS, TOK), 0)
    first, second = ids_ref[0:1, :] == expert, ids_ref[1:2, :] == expert
    member = first | second
    ordered = (
        lax.broadcasted_iota(jnp.int32, (TOK, TOK), 0)
        < lax.broadcasted_iota(jnp.int32, (TOK, TOK), 1)
    )
    before = dot_nn(
        jnp.where(member, 1.0, 0.0).astype(bf16), jnp.where(ordered, 1.0, 0.0).astype(bf16)
    )
    slot = jnp.where(member, before, -1.0)
    gate = jnp.where(first, gates_ref[0:1, :], 0.0) + jnp.where(second, gates_ref[1:2, :], 0.0)
    meta_own[...] = jnp.zeros_like(meta_own)
    for e in range(EXPERTS):
        meta_own[e, 0:1, :] = slot[e : e + 1, :]
        meta_own[e, 1:2, :] = gate[e : e + 1, :]
    meta_in[0] = meta_own[z]
    acc[...] = jnp.zeros_like(acc)

    pl.semaphore_wait(barrier, len(greeted))
    for p in range(2):
        loads[p].wait()
        start(("up", p, 1), parts[p], raw.at[0, p], ring(1))
        start(("down", p, 2), parts[p], raw.at[1, p], ring(-1))
    for i in range(1, 7):
        plane = (z - SHIFT[i] + 8) % 8
        start(("meta", i), meta_own.at[plane], meta_in.at[i], device(plane, yl, co))
    facing = meta_own.at[(z + 4) % 8]
    start(("meta", 8), facing, meta_far.at[0], ring(3))
    start(("meta", 9), facing, meta_far.at[1], ring(-3))
    start(("meta", 10), meta_own.at[(z + 3) % 8], meta_far.at[2], ring(2))
    start(("meta", 11), meta_own.at[(z + 5) % 8], meta_far.at[3], ring(-2))

    def onehot(slots):
        return slots == lax.broadcasted_iota(jnp.int32, (CAP, TOK), 0).astype(f32)

    def choose(block, meta, p):
        hot = onehot(meta[0:1, :])
        picked = dot_nn(jnp.where(hot, 1.0, 0.0).astype(bf16), block)
        if p == 1:
            weight = jnp.sum(jnp.where(hot, meta[1:2, :], 0.0), axis=1, keepdims=True)
            picked = weight * picked
        return picked.astype(bf16)

    def thin(i, p):
        return (i, p) in ((5, 1), (6, 0), (7, 0), (7, 1), (8, 1))

    def take(i, p):
        if 1 <= i <= 6 and not thin(i, p):
            name, away = ("up", 1) if i % 2 else ("down", -1)
            got = raw.at[i - 1, p]
            arrive((name, p, i), got)
            if thin(i + 2, p):
                meta = 2 if i == 3 else 3 if i == 4 else p
                arrive(("meta", 8 + meta), meta_far.at[meta])
                far_rows[meta] = choose(raw[i - 1, p], meta_far[meta], p)
                there = rows.at[p, min(i + 2, 7), mine]
                start(("thin", p, min(i + 2, 7)), far_rows.at[meta], there, ring(away))
            elif i < 5:
                start((name, p, i + 2), got, raw.at[i + 1, p], ring(away))
        if p == 0 and 1 <= i <= 6:
            arrive(("meta", i), meta_in.at[i])
        if thin(i, p):
            arrive(("thin", p, i), rows.at[p, i, mine])
        else:
            block = parts[p][...] if i == 0 else raw[i - 1, p]
            rows[p, i, mine] = choose(block, meta_in[i], p)
        chosen = rows.at[p, i, mine]
        start(("across", p, i), chosen, chosen, across)
        start(("twin", p, i), chosen, chosen, sibling)

    def pass_on(i, p):
        got = rows.at[p, i, other]
        arrive(("across", p, i), got)
        start(("forward", p, i), got, got, sibling)

    def complete(i, p):
        arrive(("twin", p, i), rows.at[p, i, twin])
        arrive(("forward", p, i), rows.at[p, i, other_twin])

    def put(i, at, value):
        value = value.reshape(2, 4, 32, HID)
        own[:, :, i, :, at : at + HID] = value
        part[:, :, i, :, at : at + HID] = value.astype(bf16)

    def multiply_x(i):
        complete(i, 0)
        block = rows[0, i].reshape(4 * CAP, FEAT)
        put(i, 0, dot_nn(block, wg_ref[...]))
        put(i, HID, dot_nn(block, wu_ref[...]))

    def multiply_c(i):
        complete(i, 1)
        put(i, 2 * HID, dot_nn(rows[1, i].reshape(4 * CAP, FEAT), wd_ref[...]))
        start(("far+", i), part.at[0, xo, i], far.at[0, i], right)
        start(("far-", i), part.at[1, xo, i], far.at[1, i], left)
        start(("own+", i), part.at[1, xp, i], near.at[0, 1, i], right)
        start(("own-", i), part.at[0, xm, i], near.at[1, 0, i], left)

    def sum_far(i):
        arrive(("far+", i), far.at[0, i])
        part[0, xp, i] = (own[0, xp, i] + far[0, i].astype(f32)).astype(bf16)
        start(("sum+", i), part.at[0, xp, i], near.at[0, 0, i], right)
        arrive(("far-", i), far.at[1, i])
        part[1, xm, i] = (own[1, xm, i] + far[1, i].astype(f32)).astype(bf16)
        start(("sum-", i), part.at[1, xm, i], near.at[1, 1, i], left)

    def sum_near(i):
        arrive(("own+", i), near.at[0, 1, i])
        arrive(("own-", i), near.at[1, 0, i])
        arrive(("sum+", i), near.at[0, 0, i])
        arrive(("sum-", i), near.at[1, 1, i])

        for half in range(2):
            total = (
                own[half, x, i] + near[0, half, i].astype(f32) + near[1, half, i].astype(f32)
            )
            keep[i, half] = total
            qsend[i, half] = total.astype(bf16)
        start(("q", i), qsend.at[i], qrecv.at[i], partner)

    def activate(i):
        arrive(("q", i), qrecv.at[i])
        for half in range(2):
            total = keep[i, half] + qrecv[i, half].astype(f32)
            a, u, g = total[:, :HID], total[:, HID : 2 * HID], total[:, 2 * HID :]
            sig = jax.nn.sigmoid(a)
            silu = a * sig
            slope = sig * (1.0 + a * (1.0 - sig))
            spread[half, x, i, :, 0:HID] = (silu * u).astype(bf16)
            spread[half, x, i, :, HID : 2 * HID] = (g * u * slope).astype(bf16)
            spread[half, x, i, :, 2 * HID : 3 * HID] = (g * silu).astype(bf16)
        for half in range(2):
            made = spread.at[half, x, i]
            start(("one+", half, i), made, made, right)
            made = spread.at[1 - half, x, i]
            start(("one-", 1 - half, i), made, made, left)

    def relay(i):
        arrive(("one+", 0, i), spread.at[0, xm, i])
        start(("on+", i), spread.at[0, xm, i], spread.at[0, xm, i], right)
        arrive(("one-", 1, i), spread.at[1, xp, i])
        start(("on-", i), spread.at[1, xp, i], spread.at[1, xp, i], left)

    def row_terms(i):
        arrive(("one+", 1, i), spread.at[1, xm, i])
        arrive(("one-", 0, i), spread.at[0, xp, i])
        arrive(("on+", i), spread.at[0, xo, i])
        arrive(("on-", i), spread.at[1, xo, i])

        def product(core):
            held = spread[:, pl.ds(2 * core, 2), i].reshape(2 * CAP, 3 * HID)
            value = dot_nt(held[:, HID : 2 * HID], wg_ref[...])
            value = value + dot_nt(held[:, 2 * HID :], wu_ref[...])
            return value.reshape(2, CAP, FEAT)

        term[i] = product(1 - co).astype(bf16)
        start(("core", i), term.at[i], term_in.at[i], sibling)
        kept[i] = product(co)

    def pair(i):
        arrive(("core", i), term_in.at[i])
        tsend[i] = (kept[i, 1 - yl] + term_in[i, 1 - yl].astype(f32)).astype(bf16)
        start(("ypair", i), tsend.at[i], trecv.at[i], across)

    def back(i):
        arrive(("ypair", i), trecv.at[i])
        value = kept[i, yl] + term_in[i, yl].astype(f32) + trecv[i].astype(f32)
        if i == 0:
            ret[0] = value.astype(bf16)
            return
        final[i] = value.astype(bf16)
        home = SHIFT.index(-SHIFT[i]) if i < 7 else 7
        start(("ret", home), final.at[i], ret.at[home], ring(SHIFT[i]))

    def weight_grads(i):
        held = spread[:, :, i].reshape(4 * CAP, 3 * HID)
        block = rows[0, i].reshape(4 * CAP, FEAT)
        acc[0] += dot_tn(held[:, HID : 2 * HID], block)
        acc[1] += dot_tn(held[:, 2 * HID :], block)
        acc[2] += dot_tn(held[:, :HID], rows[1, i].reshape(4 * CAP, FEAT))

    run = (
        lambda i: take(i, 0),
        lambda i: take(i, 1),
        lambda i: pass_on(i, 0),
        lambda i: pass_on(i, 1),
        multiply_x,
        multiply_c,
        sum_far,
        sum_near,
        activate,
        relay,
        row_terms,
        pair,
        back,
        weight_grads,
    )
    loaded = False
    for item in ORDER:
        if run[item // BLOCKS] is multiply_x and not loaded:
            for load in loads[2:]:
                load.wait()
            loaded = True
        run[item // BLOCKS](item % BLOCKS)

    stores = []
    for place, target in enumerate((gg_out, gu_out, gd_out)):
        wgrads[place] = acc[place].T.astype(bf16)
        stores.append(pltpu.make_async_copy(wgrads.at[place], target, store_sems.at[place]))
        stores[-1].start()
    hots = []
    for i in range(8):
        slots = meta_own[(z + SHIFT[i] + 8) % 8, 0:1, :]
        hots.append(jnp.where(onehot(slots), 1.0, 0.0).astype(bf16))
    hots = jnp.concatenate(hots, axis=0)
    for made in started:
        made.wait_send()
    for i in range(1, 8):
        arrive(("ret", i), ret.at[i])
    gt_ref[...] = dot_tn(hots, ret[...].reshape(8 * CAP, FEAT)).astype(bf16)
    stores.append(pltpu.make_async_copy(gt_ref, gt_out, store_sems.at[3]))
    stores[-1].start()
    for store in stores:
        store.wait()


def hand_on(*refs):
    for source, target in zip(refs[:4], refs[4:]):
        target[...] = source[...]


def body(tokens, cotangent, route_gates, expert_ids, w_gate, w_up, w_down):
    bf16, f32 = jnp.bfloat16, jnp.float32
    vmem = pl.BlockSpec(memory_space=pltpu.VMEM)
    anywhere = pl.BlockSpec(memory_space=pl.ANY)
    shape = jax.ShapeDtypeStruct
    outs = (shape((TOK, FEAT), bf16),) + (shape((FEAT, HID), bf16),) * 3
    results = pl.pallas_call(
        kernel,
        out_shape=outs,
        in_specs=[vmem] * 2 + [anywhere] * 5,
        out_specs=(anywhere,) * 4,
        scratch_shapes=[
            pltpu.VMEM((TOK, FEAT), bf16),
            pltpu.VMEM((TOK, FEAT), bf16),
            pltpu.VMEM((FEAT, HID), bf16),
            pltpu.VMEM((FEAT, HID), bf16),
            pltpu.VMEM((FEAT, HID), bf16),
            pltpu.VMEM((TOK, FEAT), bf16),
            pltpu.VMEM((3, FEAT, HID), bf16),
            pltpu.VMEM((EXPERTS, 8, TOK), f32),
            pltpu.VMEM((8, 8, TOK), f32),
            pltpu.VMEM((4, 8, TOK), f32),
            pltpu.VMEM((6, 2, TOK, FEAT), bf16),
            pltpu.VMEM((2, 8, 4, CAP, FEAT), bf16),
            pltpu.VMEM((4, CAP, FEAT), bf16),
            pltpu.VMEM((2, 4, 8, 32, 3 * HID), f32),
            pltpu.VMEM((2, 4, 8, 32, 3 * HID), bf16),
            pltpu.VMEM((2, 8, 32, 3 * HID), bf16),
            pltpu.VMEM((2, 2, 8, 32, 3 * HID), bf16),
            pltpu.VMEM((8, 2, 32, 3 * HID), f32),
            pltpu.VMEM((8, 2, 32, 3 * HID), bf16),
            pltpu.VMEM((8, 2, 32, 3 * HID), bf16),
            pltpu.VMEM((2, 4, 8, 32, 3 * HID), bf16),
            pltpu.VMEM((8, 2, CAP, FEAT), bf16),
            pltpu.VMEM((8, 2, CAP, FEAT), f32),
            pltpu.VMEM((8, 2, CAP, FEAT), bf16),
            pltpu.VMEM((8, CAP, FEAT), bf16),
            pltpu.VMEM((8, CAP, FEAT), bf16),
            pltpu.VMEM((8, CAP, FEAT), bf16),
            pltpu.VMEM((8, CAP, FEAT), bf16),
            pltpu.VMEM((3, HID, FEAT), f32),
            pltpu.SemaphoreType.DMA((SEMS,)),
            pltpu.SemaphoreType.DMA((SEMS,)),
            pltpu.SemaphoreType.DMA((5,)),
            pltpu.SemaphoreType.DMA((4,)),
        ],
        compiler_params=pltpu.CompilerParams(
            collective_id=0, has_side_effects=True, vmem_limit_bytes=60 * 1024 * 1024
        ),
    )(expert_ids.T, route_gates.T, tokens, cotangent, w_gate, w_up, w_down)
    return pl.pallas_call(
        hand_on,
        out_shape=outs,
        in_specs=[vmem] * 4,
        out_specs=(vmem,) * 4,
    )(*results)


def solution(mesh):
    placed = (
        P("ep", "fsdp"),
        P("ep", "fsdp"),
        P("ep", None),
        P("ep", None),
        P("fsdp", "ep"),
        P("fsdp", "ep"),
        P("fsdp", "ep"),
    )
    return jax.shard_map(
        body,
        mesh=mesh,
        in_specs=placed,
        out_specs=(P("ep", "fsdp"), P("fsdp", "ep"), P("fsdp", "ep"), P("fsdp", "ep")),
        check_vma=False,
    )
```

```python
import jax
import jax.numpy as jnp
from jax import lax
from jax.experimental import pallas as pl
from jax.experimental.pallas import tpu as pltpu
from jax.sharding import PartitionSpec as P

EXPERTS = 8
CAP = 64
TOK = 128
FEAT = 896
HID = 256
MESH = pl.DeviceIdType.MESH

SHIFT = (0, -1, 1, -2, 2, -3, 3, 4)
SEMS = 400

UNITS = (
    (0, 0, 64), (1, 0, 64), (2, 0, 64), (3, 0, 32), (3, 32, 32), (4, 0, 32),
    (4, 32, 32), (5, 0, 32), (5, 32, 32), (6, 0, 32), (6, 32, 32), (7, 0, 32),
    (7, 32, 32),
)

ORDER = (
    0, 13, 2, 1, 14, 15, 3, 40, 26, 39, 27, 28, 5, 41, 52, 65,
    16, 18, 54, 67, 30, 53, 66, 31, 7, 78, 43, 57, 29, 32, 80, 44,
    20, 42, 56, 69, 55, 45, 68, 9, 70, 58, 33, 22, 71, 34, 46, 59,
    81, 82, 11, 83, 35, 47, 72, 60, 36, 84, 73, 79, 48, 61, 24, 95,
    49, 74, 62, 75, 97, 37, 38, 94, 86, 85, 63, 50, 87, 96, 88, 51,
    76, 64, 77, 98, 108, 100, 110, 99, 89, 90, 107, 101, 121, 92, 123, 109,
    113, 102, 103, 93, 120, 112, 111, 136, 134, 126, 114, 122, 149, 147, 133, 91,
    125, 124, 115, 146, 116, 139, 127, 105, 135, 162, 152, 137, 160, 138, 128, 129,
    150, 106, 140, 159, 148, 118, 165, 153, 151, 104, 163, 142, 141, 119, 161, 155,
    172, 154, 131, 117, 164, 166, 144, 132, 174, 167, 168, 145, 171, 130, 143, 157,
    170, 180, 158, 176, 169, 178, 156, 182,
)


def dot_nn(left, right):
    return jnp.dot(left, right, preferred_element_type=jnp.float32)


def dot_nt(left, right):
    return lax.dot_general(
        left, right, (((1,), (1,)), ((), ())), preferred_element_type=jnp.float32
    )


def dot_tn(left, right):
    return lax.dot_general(
        left, right, (((0,), (0,)), ((), ())), preferred_element_type=jnp.float32
    )


def kernel(
    ids_ref, gates_ref, x_in, c_in, wg_in, wu_in, wd_in,
    gt_out, gg_out, gu_out, gd_out,
    x_ref, c_ref, wg_ref, wu_ref, wd_ref, gt_ref, wgrads,
    meta_own, meta_in, meta_far, raw, rows, far_rows, own, part, far, near,
    keep, qsend, qrecv, spread, term, kept, term_in, tsend, trecv, final, ret, acc, hots,
    send_sems, recv_sems, load_sems, store_sems,
):
    f32, bf16 = jnp.float32, jnp.bfloat16
    ep = lax.axis_index("ep")
    fs = lax.axis_index("fsdp")
    z, yl, co = ep // 4, (ep // 2) % 2, ep % 2
    yh, x = fs // 4, fs % 4
    xp, xm, xo = (x + 1) % 4, (x + 3) % 4, (x + 2) % 4

    def device(plane, ylo, core):
        return (plane * 4 + ylo * 2 + core, fs)

    def ring(step):
        return device((z + step + 8) % 8, yl, co)

    sibling = device(z, yl, 1 - co)
    across = device(z, 1 - yl, co)
    right, left = (ep, yh * 4 + xp), (ep, yh * 4 + xm)
    partner = (ep, (1 - yh) * 4 + x)
    mine, twin = yl * 2 + co, yl * 2 + (1 - co)
    other, other_twin = (1 - yl) * 2 + co, (1 - yl) * 2 + (1 - co)

    places = {}
    started = []

    def copy(name, source, target, where):
        place = places.setdefault(name, len(places))
        return pltpu.make_async_remote_copy(
            src_ref=source,
            dst_ref=target,
            send_sem=send_sems.at[place],
            recv_sem=recv_sems.at[place],
            device_id=where,
            device_id_type=MESH,
        )

    def start(name, source, target, where):
        made = copy(name, source, target, where)
        made.start()
        started.append(made)

    def arrive(name, target):
        copy(name, target, target, sibling).wait_recv()

    barrier = pltpu.get_barrier_semaphore()
    greeted = [ring(step) for step in range(1, 8)] + [sibling, across, right, left, partner]
    for where in greeted:
        pl.semaphore_signal(barrier, inc=1, device_id=where, device_id_type=MESH)

    loads = [
        pltpu.make_async_copy(source, target, load_sems.at[place])
        for place, (source, target) in enumerate(
            ((x_in, x_ref), (c_in, c_ref), (wg_in, wg_ref), (wu_in, wu_ref), (wd_in, wd_ref))
        )
    ]
    for load in loads:
        load.start()
    parts = (x_ref, c_ref)

    pl.semaphore_wait(barrier, len(greeted))
    for p in range(2):
        loads[p].wait()
        start(("up", p, 1), parts[p], raw.at[0, p], ring(1))
        start(("down", p, 2), parts[p], raw.at[1, p], ring(-1))

    expert = lax.broadcasted_iota(jnp.int32, (EXPERTS, TOK), 0)
    first, second = ids_ref[0:1, :] == expert, ids_ref[1:2, :] == expert
    member = first | second
    ordered = (
        lax.broadcasted_iota(jnp.int32, (TOK, TOK), 0)
        < lax.broadcasted_iota(jnp.int32, (TOK, TOK), 1)
    )
    before = dot_nn(
        jnp.where(member, 1.0, 0.0).astype(bf16), jnp.where(ordered, 1.0, 0.0).astype(bf16)
    )
    slot = jnp.where(member, before, -1.0)
    gate = jnp.where(first, gates_ref[0:1, :], 0.0) + jnp.where(second, gates_ref[1:2, :], 0.0)
    meta_own[...] = jnp.zeros_like(meta_own)
    for e in range(EXPERTS):
        meta_own[e, 0:1, :] = slot[e : e + 1, :]
        meta_own[e, 1:2, :] = gate[e : e + 1, :]
    meta_in[0] = meta_own[z]
    for i in range(1, 7):
        plane = (z - SHIFT[i] + 8) % 8
        start(("meta", i), meta_own.at[plane], meta_in.at[i], device(plane, yl, co))
    facing = meta_own.at[(z + 4) % 8]
    start(("meta", 8), facing, meta_far.at[0], ring(3))
    start(("meta", 9), facing, meta_far.at[1], ring(-3))
    start(("meta", 10), meta_own.at[(z + 3) % 8], meta_far.at[2], ring(2))
    start(("meta", 11), meta_own.at[(z + 5) % 8], meta_far.at[3], ring(-2))

    def onehot(slots):
        return slots == lax.broadcasted_iota(jnp.int32, (CAP, TOK), 0).astype(f32)

    acc[...] = jnp.zeros_like(acc)
    for i in range(8):
        slots = meta_own[(z + SHIFT[i] + 8) % 8, 0:1, :]
        hots[:, i * CAP : (i + 1) * CAP] = jnp.where(onehot(slots), 1.0, 0.0).T.astype(bf16)

    def choose(block, meta, p):
        hot = onehot(meta[0:1, :])
        picked = dot_nn(jnp.where(hot, 1.0, 0.0).astype(bf16), block)
        if p == 1:
            weight = jnp.sum(jnp.where(hot, meta[1:2, :], 0.0), axis=1, keepdims=True)
            picked = weight * picked
        return picked.astype(bf16)

    def thin(i, p):
        return (i, p) in ((5, 1), (6, 0), (7, 0), (7, 1), (8, 1))

    def span(u):
        i, low, count = UNITS[u]
        return i, pl.ds(low, count), pl.ds(low // 2, count // 2)

    def units_of(i):
        return [u for u, unit in enumerate(UNITS) if unit[0] == i]

    def take(u, p):
        i = UNITS[u][0]
        if 1 <= i <= 6 and not thin(i, p):
            name, away = ("up", 1) if i % 2 else ("down", -1)
            got = raw.at[i - 1, p]
            arrive((name, p, i), got)
            if thin(i + 2, p):
                meta = 2 if i == 3 else 3 if i == 4 else p
                arrive(("meta", 8 + meta), meta_far.at[meta])
                far_rows[meta] = choose(raw[i - 1, p], meta_far[meta], p)
                there = rows.at[p, min(i + 2, 7), mine]
                start(("thin", p, min(i + 2, 7)), far_rows.at[meta], there, ring(away))
            elif i < 5:
                start((name, p, i + 2), got, raw.at[i + 1, p], ring(away))
        if p == 0 and 1 <= i <= 6:
            arrive(("meta", i), meta_in.at[i])
        if thin(i, p):
            arrive(("thin", p, i), rows.at[p, i, mine])
        else:
            block = parts[p][...] if i == 0 else raw[i - 1, p]
            rows[p, i, mine] = choose(block, meta_in[i], p)
        for v in units_of(i):
            chosen = rows.at[p, i, mine, span(v)[1]]
            start(("across", p, v), chosen, chosen, across)
            start(("twin", p, v), chosen, chosen, sibling)

    def pass_on(u, p):
        i, slots, _ = span(u)
        got = rows.at[p, i, other, slots]
        arrive(("across", p, u), got)
        start(("forward", p, u), got, got, sibling)

    def complete(u, p):
        i, slots, _ = span(u)
        arrive(("twin", p, u), rows.at[p, i, twin, slots])
        arrive(("forward", p, u), rows.at[p, i, other_twin, slots])

    def block_rows(u, p):
        i, slots, _ = span(u)
        return rows[p, i, :, slots, :].reshape(4 * UNITS[u][2], FEAT)

    def put(u, at, value):
        i, _, q = span(u)
        value = value.reshape(2, 4, UNITS[u][2] // 2, HID)
        own[:, :, i, q, at : at + HID] = value
        part[:, :, i, q, at : at + HID] = value.astype(bf16)

    def multiply_x(u):
        complete(u, 0)
        block = block_rows(u, 0)
        put(u, 0, dot_nn(block, wg_ref[...]))
        put(u, HID, dot_nn(block, wu_ref[...]))

    def multiply_c(u):
        complete(u, 1)
        i, _, q = span(u)
        put(u, 2 * HID, dot_nn(block_rows(u, 1), wd_ref[...]))
        start(("far+", u), part.at[0, xo, i, q], far.at[0, i, q], right)
        start(("far-", u), part.at[1, xo, i, q], far.at[1, i, q], left)
        start(("own+", u), part.at[1, xp, i, q], near.at[0, 1, i, q], right)
        start(("own-", u), part.at[0, xm, i, q], near.at[1, 0, i, q], left)

    def sum_far(u):
        i, _, q = span(u)
        arrive(("far+", u), far.at[0, i, q])
        part[0, xp, i, q] = (own[0, xp, i, q] + far[0, i, q].astype(f32)).astype(bf16)
        start(("sum+", u), part.at[0, xp, i, q], near.at[0, 0, i, q], right)
        arrive(("far-", u), far.at[1, i, q])
        part[1, xm, i, q] = (own[1, xm, i, q] + far[1, i, q].astype(f32)).astype(bf16)
        start(("sum-", u), part.at[1, xm, i, q], near.at[1, 1, i, q], left)

    def sum_near(u):
        i, _, q = span(u)
        arrive(("own+", u), near.at[0, 1, i, q])
        arrive(("own-", u), near.at[1, 0, i, q])
        arrive(("sum+", u), near.at[0, 0, i, q])
        arrive(("sum-", u), near.at[1, 1, i, q])
        for half in range(2):
            total = (
                own[half, x, i, q]
                + near[0, half, i, q].astype(f32)
                + near[1, half, i, q].astype(f32)
            )
            keep[i, half, q] = total
            qsend[i, half, q] = total.astype(bf16)
        start(("q", u), qsend.at[i, :, q], qrecv.at[i, :, q], partner)

    def activate(u):
        i, _, q = span(u)
        arrive(("q", u), qrecv.at[i, :, q])
        for half in range(2):
            total = keep[i, half, q] + qrecv[i, half, q].astype(f32)
            a, up, g = total[:, :HID], total[:, HID : 2 * HID], total[:, 2 * HID :]
            sig = jax.nn.sigmoid(a)
            silu = a * sig
            slope = sig * (1.0 + a * (1.0 - sig))
            spread[half, x, i, q, 0:HID] = (silu * up).astype(bf16)
            spread[half, x, i, q, HID : 2 * HID] = (g * up * slope).astype(bf16)
            spread[half, x, i, q, 2 * HID : 3 * HID] = (g * silu).astype(bf16)
        for half in range(2):
            made = spread.at[half, x, i, q]
            start(("one+", half, u), made, made, right)
            made = spread.at[1 - half, x, i, q]
            start(("one-", 1 - half, u), made, made, left)

    def relay(u):
        i, _, q = span(u)
        got = spread.at[0, xm, i, q]
        arrive(("one+", 0, u), got)
        start(("on+", u), got, got, right)
        got = spread.at[1, xp, i, q]
        arrive(("one-", 1, u), got)
        start(("on-", u), got, got, left)

    def row_terms(u):
        i, slots, q = span(u)
        arrive(("one+", 1, u), spread.at[1, xm, i, q])
        arrive(("one-", 0, u), spread.at[0, xp, i, q])
        arrive(("on+", u), spread.at[0, xo, i, q])
        arrive(("on-", u), spread.at[1, xo, i, q])
        count = UNITS[u][2]

        def product(core):
            held = spread[:, pl.ds(2 * core, 2), i, q].reshape(2 * count, 3 * HID)
            value = dot_nt(held[:, HID : 2 * HID], wg_ref[...])
            value = value + dot_nt(held[:, 2 * HID :], wu_ref[...])
            return value.reshape(2, count, FEAT)

        term[i, :, slots] = product(1 - co).astype(bf16)
        start(("core", u), term.at[i, :, slots], term_in.at[i, :, slots], sibling)
        kept[i, :, slots] = product(co)

    def pair(u):
        i, slots, _ = span(u)
        arrive(("core", u), term_in.at[i, :, slots])
        tsend[i, slots] = (
            kept[i, 1 - yl, slots] + term_in[i, 1 - yl, slots].astype(f32)
        ).astype(bf16)
        start(("ypair", u), tsend.at[i, slots], trecv.at[i, slots], across)

    def back(u):
        i, slots, _ = span(u)
        arrive(("ypair", u), trecv.at[i, slots])
        value = kept[i, yl, slots] + term_in[i, yl, slots].astype(f32)
        value = (value + trecv[i, slots].astype(f32)).astype(bf16)
        if i == 0:
            ret[0, slots] = value
            return
        final[i, slots] = value
        home = SHIFT.index(-SHIFT[i]) if i < 7 else 7
        name = ("ret", home, UNITS[u][1])
        start(name, final.at[i, slots], ret.at[home, slots], ring(SHIFT[i]))

    def weight_grads(u):
        i = UNITS[u][0]

        def joined(pieces):
            return pieces[0] if len(pieces) == 1 else jnp.concatenate(pieces, axis=0)

        own_units = units_of(i)
        held = joined(
            [spread[:, :, i, span(v)[2]].reshape(4 * UNITS[v][2], 3 * HID) for v in own_units]
        )
        block = joined([block_rows(v, 0) for v in own_units])
        acc[0] += dot_tn(held[:, HID : 2 * HID], block)
        acc[1] += dot_tn(held[:, 2 * HID :], block)
        acc[2] += dot_tn(held[:, :HID], joined([block_rows(v, 1) for v in own_units]))

    stores = []

    def finish(_):
        for place, target in enumerate((gg_out, gu_out, gd_out)):
            wgrads[place] = acc[place].T.astype(bf16)
            stores.append(pltpu.make_async_copy(wgrads.at[place], target, store_sems.at[place]))
            stores[-1].start()

    run = (
        lambda u: take(u, 0),
        lambda u: take(u, 1),
        lambda u: pass_on(u, 0),
        lambda u: pass_on(u, 1),
        multiply_x,
        multiply_c,
        sum_far,
        sum_near,
        activate,
        relay,
        row_terms,
        pair,
        back,
        weight_grads,
        finish,
    )
    loaded = False
    for item in ORDER:
        step, u = item // len(UNITS), item % len(UNITS)
        if run[step] is multiply_x and not loaded:
            for load in loads[2:]:
                load.wait()
            loaded = True
        run[step](u)

    for made in started:
        made.wait_send()
    for i, low, count in UNITS:
        if i > 0:
            arrive(("ret", i, low), ret.at[i, pl.ds(low, count)])
    gt_ref[...] = dot_nn(hots[...], ret[...].reshape(8 * CAP, FEAT)).astype(bf16)
    stores.append(pltpu.make_async_copy(gt_ref, gt_out, store_sems.at[3]))
    stores[-1].start()
    for store in stores:
        store.wait()


def hand_on(*refs):
    sems = refs[8]
    copies = [pltpu.make_async_copy(refs[k], refs[4 + k], sems.at[k]) for k in range(4)]
    for item in copies:
        item.start()
    for item in copies:
        item.wait()


def body(tokens, cotangent, route_gates, expert_ids, w_gate, w_up, w_down):
    bf16, f32 = jnp.bfloat16, jnp.float32
    vmem = pl.BlockSpec(memory_space=pltpu.VMEM)
    anywhere = pl.BlockSpec(memory_space=pl.ANY)
    shape = jax.ShapeDtypeStruct
    outs = (shape((TOK, FEAT), bf16),) + (shape((FEAT, HID), bf16),) * 3
    results = pl.pallas_call(
        kernel,
        out_shape=outs,
        in_specs=[vmem] * 2 + [anywhere] * 5,
        out_specs=(anywhere,) * 4,
        scratch_shapes=[
            pltpu.VMEM((TOK, FEAT), bf16),
            pltpu.VMEM((TOK, FEAT), bf16),
            pltpu.VMEM((FEAT, HID), bf16),
            pltpu.VMEM((FEAT, HID), bf16),
            pltpu.VMEM((FEAT, HID), bf16),
            pltpu.VMEM((TOK, FEAT), bf16),
            pltpu.VMEM((3, FEAT, HID), bf16),
            pltpu.VMEM((EXPERTS, 8, TOK), f32),
            pltpu.VMEM((8, 8, TOK), f32),
            pltpu.VMEM((4, 8, TOK), f32),
            pltpu.VMEM((6, 2, TOK, FEAT), bf16),
            pltpu.VMEM((2, 8, 4, CAP, FEAT), bf16),
            pltpu.VMEM((4, CAP, FEAT), bf16),
            pltpu.VMEM((2, 4, 8, 32, 3 * HID), f32),
            pltpu.VMEM((2, 4, 8, 32, 3 * HID), bf16),
            pltpu.VMEM((2, 8, 32, 3 * HID), bf16),
            pltpu.VMEM((2, 2, 8, 32, 3 * HID), bf16),
            pltpu.VMEM((8, 2, 32, 3 * HID), f32),
            pltpu.VMEM((8, 2, 32, 3 * HID), bf16),
            pltpu.VMEM((8, 2, 32, 3 * HID), bf16),
            pltpu.VMEM((2, 4, 8, 32, 3 * HID), bf16),
            pltpu.VMEM((8, 2, CAP, FEAT), bf16),
            pltpu.VMEM((8, 2, CAP, FEAT), f32),
            pltpu.VMEM((8, 2, CAP, FEAT), bf16),
            pltpu.VMEM((8, CAP, FEAT), bf16),
            pltpu.VMEM((8, CAP, FEAT), bf16),
            pltpu.VMEM((8, CAP, FEAT), bf16),
            pltpu.VMEM((8, CAP, FEAT), bf16),
            pltpu.VMEM((3, HID, FEAT), f32),
            pltpu.VMEM((TOK, 8 * CAP), bf16),
            pltpu.SemaphoreType.DMA((SEMS,)),
            pltpu.SemaphoreType.DMA((SEMS,)),
            pltpu.SemaphoreType.DMA((5,)),
            pltpu.SemaphoreType.DMA((4,)),
        ],
        compiler_params=pltpu.CompilerParams(
            collective_id=0, has_side_effects=True, vmem_limit_bytes=60 * 1024 * 1024
        ),
    )(expert_ids.T, route_gates.T, tokens, cotangent, w_gate, w_up, w_down)
    return pl.pallas_call(
        hand_on,
        out_shape=outs,
        in_specs=[anywhere] * 4,
        out_specs=(vmem,) * 4,
        scratch_shapes=[pltpu.SemaphoreType.DMA((4,))],
    )(*results)


def solution(mesh):
    placed = (
        P("ep", "fsdp"),
        P("ep", "fsdp"),
        P("ep", None),
        P("ep", None),
        P("fsdp", "ep"),
        P("fsdp", "ep"),
        P("fsdp", "ep"),
    )
    return jax.shard_map(
        body,
        mesh=mesh,
        in_specs=placed,
        out_specs=(P("ep", "fsdp"), P("fsdp", "ep"), P("fsdp", "ep"), P("fsdp", "ep")),
        check_vma=False,
    )
```

```python
import jax
import jax.numpy as jnp
from jax import lax
from jax.experimental import pallas as pl
from jax.experimental.pallas import tpu as pltpu
from jax.sharding import PartitionSpec as P

EXPERTS = 8
CAP = 64
TOK = 128
FEAT = 896
HID = 256
MESH = pl.DeviceIdType.MESH

SHIFT = (0, -1, 1, -2, 2, -3, 3, 4)
BLOCKS = 8
SEMS = 288

ORDER = (
    0, 8, 1, 16, 2, 24, 9, 10, 32, 40, 18, 3, 4, 25, 34, 26,
    17, 12, 42, 11, 33, 41, 6, 5, 20, 28, 19, 50, 36, 44, 27, 14,
    35, 43, 13, 22, 48, 49, 52, 21, 7, 15, 30, 51, 38, 46, 29, 37,
    45, 23, 59, 60, 54, 39, 31, 58, 53, 47, 62, 67, 61, 55, 68, 75,
    56, 70, 63, 76, 69, 57, 83, 78, 91, 84, 77, 71, 92, 86, 65, 94,
    85, 79, 99, 66, 93, 100, 73, 64, 102, 87, 111, 74, 101, 95, 81, 72,
    89, 82, 106, 103, 90, 80, 107, 88, 108, 97, 110, 98, 96, 109, 105, 104,
)


def dot_nn(left, right):
    return jnp.dot(left, right, preferred_element_type=jnp.float32)


def dot_nt(left, right):
    return lax.dot_general(
        left, right, (((1,), (1,)), ((), ())), preferred_element_type=jnp.float32
    )


def dot_tn(left, right):
    return lax.dot_general(
        left, right, (((0,), (0,)), ((), ())), preferred_element_type=jnp.float32
    )


def kernel(
    ids_ref, gates_ref, x_in, c_in, wg_in, wu_in, wd_in,
    ret_out, hot_out, gg_out, gu_out, gd_out,
    x_ref, c_ref, wg_ref, wu_ref, wd_ref, hot_ref, wgrads,
    meta_own, meta_in, meta_far, raw, rows, far_rows, own, part, far, near,
    keep, qsend, qrecv, spread, term, kept, term_in, tsend, trecv, final, ret, acc,
    send_sems, recv_sems, load_sems, store_sems,
):
    f32, bf16 = jnp.float32, jnp.bfloat16
    ep = lax.axis_index("ep")
    fs = lax.axis_index("fsdp")
    z, yl, co = ep // 4, (ep // 2) % 2, ep % 2
    yh, x = fs // 4, fs % 4
    xp, xm, xo = (x + 1) % 4, (x + 3) % 4, (x + 2) % 4

    def device(plane, ylo, core):
        return (plane * 4 + ylo * 2 + core, fs)

    def ring(step):
        return device((z + step + 8) % 8, yl, co)

    sibling = device(z, yl, 1 - co)
    across = device(z, 1 - yl, co)
    right, left = (ep, yh * 4 + xp), (ep, yh * 4 + xm)
    partner = (ep, (1 - yh) * 4 + x)
    mine, twin = yl * 2 + co, yl * 2 + (1 - co)
    other, other_twin = (1 - yl) * 2 + co, (1 - yl) * 2 + (1 - co)

    places = {}
    started = []

    def copy(name, source, target, where):
        place = places.setdefault(name, len(places))
        return pltpu.make_async_remote_copy(
            src_ref=source,
            dst_ref=target,
            send_sem=send_sems.at[place],
            recv_sem=recv_sems.at[place],
            device_id=where,
            device_id_type=MESH,
        )

    def start(name, source, target, where):
        made = copy(name, source, target, where)
        made.start()
        started.append(made)

    def arrive(name, target):
        copy(name, target, target, sibling).wait_recv()

    barrier = pltpu.get_barrier_semaphore()
    greeted = [ring(step) for step in range(1, 8)] + [sibling, across, right, left, partner]
    for where in greeted:
        pl.semaphore_signal(barrier, inc=1, device_id=where, device_id_type=MESH)

    loads = [
        pltpu.make_async_copy(source, target, load_sems.at[place])
        for place, (source, target) in enumerate(
            ((x_in, x_ref), (c_in, c_ref), (wg_in, wg_ref), (wu_in, wu_ref), (wd_in, wd_ref))
        )
    ]
    for load in loads:
        load.start()
    parts = (x_ref, c_ref)

    expert = lax.broadcasted_iota(jnp.int32, (EXPERTS, TOK), 0)
    first, second = ids_ref[0:1, :] == expert, ids_ref[1:2, :] == expert
    member = first | second
    ordered = (
        lax.broadcasted_iota(jnp.int32, (TOK, TOK), 0)
        < lax.broadcasted_iota(jnp.int32, (TOK, TOK), 1)
    )
    before = dot_nn(
        jnp.where(member, 1.0, 0.0).astype(bf16), jnp.where(ordered, 1.0, 0.0).astype(bf16)
    )
    slot = jnp.where(member, before, -1.0)
    gate = jnp.where(first, gates_ref[0:1, :], 0.0) + jnp.where(second, gates_ref[1:2, :], 0.0)
    meta_own[...] = jnp.zeros_like(meta_own)
    for e in range(EXPERTS):
        meta_own[e, 0:1, :] = slot[e : e + 1, :]
        meta_own[e, 1:2, :] = gate[e : e + 1, :]
    meta_in[0] = meta_own[z]
    acc[...] = jnp.zeros_like(acc)

    pl.semaphore_wait(barrier, len(greeted))
    for p in range(2):
        loads[p].wait()
        start(("up", p, 1), parts[p], raw.at[0, p], ring(1))
        start(("down", p, 2), parts[p], raw.at[1, p], ring(-1))
    for i in range(1, 7):
        plane = (z - SHIFT[i] + 8) % 8
        start(("meta", i), meta_own.at[plane], meta_in.at[i], device(plane, yl, co))
    facing = meta_own.at[(z + 4) % 8]
    start(("meta", 8), facing, meta_far.at[0], ring(3))
    start(("meta", 9), facing, meta_far.at[1], ring(-3))
    start(("meta", 10), meta_own.at[(z + 3) % 8], meta_far.at[2], ring(2))
    start(("meta", 11), meta_own.at[(z + 5) % 8], meta_far.at[3], ring(-2))

    def onehot(slots):
        return slots == lax.broadcasted_iota(jnp.int32, (CAP, TOK), 0).astype(f32)

    def choose(block, meta, p):
        hot = onehot(meta[0:1, :])
        picked = dot_nn(jnp.where(hot, 1.0, 0.0).astype(bf16), block)
        if p == 1:
            weight = jnp.sum(jnp.where(hot, meta[1:2, :], 0.0), axis=1, keepdims=True)
            picked = weight * picked
        return picked.astype(bf16)

    def thin(i, p):
        return (i, p) in ((5, 1), (6, 0), (7, 0), (7, 1), (8, 1))

    def take(i, p):
        if 1 <= i <= 6 and not thin(i, p):
            name, away = ("up", 1) if i % 2 else ("down", -1)
            got = raw.at[i - 1, p]
            arrive((name, p, i), got)
            if thin(i + 2, p):
                meta = 2 if i == 3 else 3 if i == 4 else p
                arrive(("meta", 8 + meta), meta_far.at[meta])
                far_rows[meta] = choose(raw[i - 1, p], meta_far[meta], p)
                there = rows.at[p, min(i + 2, 7), mine]
                start(("thin", p, min(i + 2, 7)), far_rows.at[meta], there, ring(away))
            elif i < 5:
                start((name, p, i + 2), got, raw.at[i + 1, p], ring(away))
        if p == 0 and 1 <= i <= 6:
            arrive(("meta", i), meta_in.at[i])
        if thin(i, p):
            arrive(("thin", p, i), rows.at[p, i, mine])
        else:
            block = parts[p][...] if i == 0 else raw[i - 1, p]
            rows[p, i, mine] = choose(block, meta_in[i], p)
        chosen = rows.at[p, i, mine]
        start(("across", p, i), chosen, chosen, across)
        start(("twin", p, i), chosen, chosen, sibling)

    def pass_on(i, p):
        got = rows.at[p, i, other]
        arrive(("across", p, i), got)
        start(("forward", p, i), got, got, sibling)

    def complete(i, p):
        arrive(("twin", p, i), rows.at[p, i, twin])
        arrive(("forward", p, i), rows.at[p, i, other_twin])

    def put(i, at, value):
        value = value.reshape(2, 4, 32, HID)
        own[:, :, i, :, at : at + HID] = value
        part[:, :, i, :, at : at + HID] = value.astype(bf16)

    def multiply_x(i):
        complete(i, 0)
        block = rows[0, i].reshape(4 * CAP, FEAT)
        put(i, 0, dot_nn(block, wg_ref[...]))
        put(i, HID, dot_nn(block, wu_ref[...]))

    def multiply_c(i):
        complete(i, 1)
        put(i, 2 * HID, dot_nn(rows[1, i].reshape(4 * CAP, FEAT), wd_ref[...]))
        start(("far+", i), part.at[0, xo, i], far.at[0, i], right)
        start(("far-", i), part.at[1, xo, i], far.at[1, i], left)
        start(("own+", i), part.at[1, xp, i], near.at[0, 1, i], right)
        start(("own-", i), part.at[0, xm, i], near.at[1, 0, i], left)

    def sum_far(i):
        arrive(("far+", i), far.at[0, i])
        part[0, xp, i] = (own[0, xp, i] + far[0, i].astype(f32)).astype(bf16)
        start(("sum+", i), part.at[0, xp, i], near.at[0, 0, i], right)
        arrive(("far-", i), far.at[1, i])
        part[1, xm, i] = (own[1, xm, i] + far[1, i].astype(f32)).astype(bf16)
        start(("sum-", i), part.at[1, xm, i], near.at[1, 1, i], left)

    def sum_near(i):
        arrive(("own+", i), near.at[0, 1, i])
        arrive(("own-", i), near.at[1, 0, i])
        arrive(("sum+", i), near.at[0, 0, i])
        arrive(("sum-", i), near.at[1, 1, i])

        for half in range(2):
            total = (
                own[half, x, i] + near[0, half, i].astype(f32) + near[1, half, i].astype(f32)
            )
            keep[i, half] = total
            qsend[i, half] = total.astype(bf16)
        start(("q", i), qsend.at[i], qrecv.at[i], partner)

    def activate(i):
        arrive(("q", i), qrecv.at[i])
        for half in range(2):
            total = keep[i, half] + qrecv[i, half].astype(f32)
            a, u, g = total[:, :HID], total[:, HID : 2 * HID], total[:, 2 * HID :]
            sig = jax.nn.sigmoid(a)
            silu = a * sig
            slope = sig * (1.0 + a * (1.0 - sig))
            spread[half, x, i, :, 0:HID] = (silu * u).astype(bf16)
            spread[half, x, i, :, HID : 2 * HID] = (g * u * slope).astype(bf16)
            spread[half, x, i, :, 2 * HID : 3 * HID] = (g * silu).astype(bf16)
        for half in range(2):
            made = spread.at[half, x, i]
            start(("one+", half, i), made, made, right)
            made = spread.at[1 - half, x, i]
            start(("one-", 1 - half, i), made, made, left)

    def relay(i):
        arrive(("one+", 0, i), spread.at[0, xm, i])
        start(("on+", i), spread.at[0, xm, i], spread.at[0, xm, i], right)
        arrive(("one-", 1, i), spread.at[1, xp, i])
        start(("on-", i), spread.at[1, xp, i], spread.at[1, xp, i], left)

    def row_terms(i):
        arrive(("one+", 1, i), spread.at[1, xm, i])
        arrive(("one-", 0, i), spread.at[0, xp, i])
        arrive(("on+", i), spread.at[0, xo, i])
        arrive(("on-", i), spread.at[1, xo, i])

        def product(core):
            held = spread[:, pl.ds(2 * core, 2), i].reshape(2 * CAP, 3 * HID)
            value = dot_nt(held[:, HID : 2 * HID], wg_ref[...])
            value = value + dot_nt(held[:, 2 * HID :], wu_ref[...])
            return value.reshape(2, CAP, FEAT)

        term[i] = product(1 - co).astype(bf16)
        start(("core", i), term.at[i], term_in.at[i], sibling)
        kept[i] = product(co)

    def pair(i):
        arrive(("core", i), term_in.at[i])
        tsend[i] = (kept[i, 1 - yl] + term_in[i, 1 - yl].astype(f32)).astype(bf16)
        start(("ypair", i), tsend.at[i], trecv.at[i], across)

    def back(i):
        arrive(("ypair", i), trecv.at[i])
        value = kept[i, yl] + term_in[i, yl].astype(f32) + trecv[i].astype(f32)
        if i == 0:
            ret[0] = value.astype(bf16)
            return
        final[i] = value.astype(bf16)
        home = SHIFT.index(-SHIFT[i]) if i < 7 else 7
        start(("ret", home), final.at[i], ret.at[home], ring(SHIFT[i]))

    def weight_grads(i):
        held = spread[:, :, i].reshape(4 * CAP, 3 * HID)
        block = rows[0, i].reshape(4 * CAP, FEAT)
        acc[0] += dot_tn(held[:, HID : 2 * HID], block)
        acc[1] += dot_tn(held[:, 2 * HID :], block)
        acc[2] += dot_tn(held[:, :HID], rows[1, i].reshape(4 * CAP, FEAT))

    run = (
        lambda i: take(i, 0),
        lambda i: take(i, 1),
        lambda i: pass_on(i, 0),
        lambda i: pass_on(i, 1),
        multiply_x,
        multiply_c,
        sum_far,
        sum_near,
        activate,
        relay,
        row_terms,
        pair,
        back,
        weight_grads,
    )
    loaded = False
    for item in ORDER:
        if run[item // BLOCKS] is multiply_x and not loaded:
            for load in loads[2:]:
                load.wait()
            loaded = True
        run[item // BLOCKS](item % BLOCKS)

    stores = []
    for place, target in enumerate((gg_out, gu_out, gd_out)):
        wgrads[place] = acc[place].T.astype(bf16)
        stores.append(pltpu.make_async_copy(wgrads.at[place], target, store_sems.at[place]))
        stores[-1].start()
    hots = []
    for i in range(8):
        slots = meta_own[(z + SHIFT[i] + 8) % 8, 0:1, :]
        hots.append(jnp.where(onehot(slots), 1.0, 0.0).astype(bf16))
    hot_ref[...] = jnp.concatenate(hots, axis=0)
    stores.append(pltpu.make_async_copy(hot_ref, hot_out, store_sems.at[3]))
    stores[-1].start()
    for made in started:
        made.wait_send()
    for i in range(8):
        if i > 0:
            arrive(("ret", i), ret.at[i])
        stores.append(pltpu.make_async_copy(ret.at[i], ret_out.at[i], store_sems.at[4 + i]))
        stores[-1].start()
    for store in stores:
        store.wait()


def combine(ret, hot, gg, gu, gd, gt_out, gg_out, gu_out, gd_out):
    gt_out[...] = dot_tn(hot[...], ret[...].reshape(8 * CAP, FEAT)).astype(jnp.bfloat16)
    for source, target in ((gg, gg_out), (gu, gu_out), (gd, gd_out)):
        target[...] = source[...]


def body(tokens, cotangent, route_gates, expert_ids, w_gate, w_up, w_down):
    bf16, f32 = jnp.bfloat16, jnp.float32
    vmem = pl.BlockSpec(memory_space=pltpu.VMEM)
    anywhere = pl.BlockSpec(memory_space=pl.ANY)
    shape = jax.ShapeDtypeStruct
    outs = (shape((TOK, FEAT), bf16),) + (shape((FEAT, HID), bf16),) * 3
    sent = (shape((8, CAP, FEAT), bf16), shape((8 * CAP, TOK), bf16)) + outs[1:]
    results = pl.pallas_call(
        kernel,
        out_shape=sent,
        in_specs=[vmem] * 2 + [anywhere] * 5,
        out_specs=(anywhere,) * 5,
        scratch_shapes=[
            pltpu.VMEM((TOK, FEAT), bf16),
            pltpu.VMEM((TOK, FEAT), bf16),
            pltpu.VMEM((FEAT, HID), bf16),
            pltpu.VMEM((FEAT, HID), bf16),
            pltpu.VMEM((FEAT, HID), bf16),
            pltpu.VMEM((8 * CAP, TOK), bf16),
            pltpu.VMEM((3, FEAT, HID), bf16),
            pltpu.VMEM((EXPERTS, 8, TOK), f32),
            pltpu.VMEM((8, 8, TOK), f32),
            pltpu.VMEM((4, 8, TOK), f32),
            pltpu.VMEM((6, 2, TOK, FEAT), bf16),
            pltpu.VMEM((2, 8, 4, CAP, FEAT), bf16),
            pltpu.VMEM((4, CAP, FEAT), bf16),
            pltpu.VMEM((2, 4, 8, 32, 3 * HID), f32),
            pltpu.VMEM((2, 4, 8, 32, 3 * HID), bf16),
            pltpu.VMEM((2, 8, 32, 3 * HID), bf16),
            pltpu.VMEM((2, 2, 8, 32, 3 * HID), bf16),
            pltpu.VMEM((8, 2, 32, 3 * HID), f32),
            pltpu.VMEM((8, 2, 32, 3 * HID), bf16),
            pltpu.VMEM((8, 2, 32, 3 * HID), bf16),
            pltpu.VMEM((2, 4, 8, 32, 3 * HID), bf16),
            pltpu.VMEM((8, 2, CAP, FEAT), bf16),
            pltpu.VMEM((8, 2, CAP, FEAT), f32),
            pltpu.VMEM((8, 2, CAP, FEAT), bf16),
            pltpu.VMEM((8, CAP, FEAT), bf16),
            pltpu.VMEM((8, CAP, FEAT), bf16),
            pltpu.VMEM((8, CAP, FEAT), bf16),
            pltpu.VMEM((8, CAP, FEAT), bf16),
            pltpu.VMEM((3, HID, FEAT), f32),
            pltpu.SemaphoreType.DMA((SEMS,)),
            pltpu.SemaphoreType.DMA((SEMS,)),
            pltpu.SemaphoreType.DMA((5,)),
            pltpu.SemaphoreType.DMA((12,)),
        ],
        compiler_params=pltpu.CompilerParams(
            collective_id=0, has_side_effects=True, vmem_limit_bytes=60 * 1024 * 1024
        ),
    )(expert_ids.T, route_gates.T, tokens, cotangent, w_gate, w_up, w_down)
    return pl.pallas_call(
        combine,
        out_shape=outs,
        in_specs=[vmem] * 5,
        out_specs=(vmem,) * 4,
    )(*results)


def solution(mesh):
    placed = (
        P("ep", "fsdp"),
        P("ep", "fsdp"),
        P("ep", None),
        P("ep", None),
        P("fsdp", "ep"),
        P("fsdp", "ep"),
        P("fsdp", "ep"),
    )
    return jax.shard_map(
        body,
        mesh=mesh,
        in_specs=placed,
        out_specs=(P("ep", "fsdp"), P("fsdp", "ep"), P("fsdp", "ep"), P("fsdp", "ep")),
        check_vma=False,
    )
```
